512 devices in a mesh: prow: 32 (over z, x), pcol: 16 (over y, core).
Axes of the slice: x: 4, y: 8, z: 8, core: 2. Of those that a mesh axis runs over, the one named last changes fastest.
Arguments:
- matrix: float32 [16384, 6144], P('prow', 'pcol'), may hold values from -6 to 6
- panel: float32 [16384, 512], P('prow', 'pcol'), may hold values from -0.25 to 0.25
- sources: int32 [512], replicated, may hold values from 0 to 16383, as said below
Outputs:
- updated: float32 [16384, 6144], P('prow', 'pcol')
The draws below stay inside these ranges and needn't reach their ends.
Inputs may be any that keep to these rules, and one draw needn't show every extreme that they name: `sources`: the entries are distinct; one equals 16383 and another equals 8192.
All inputs are finite; a program needn't handle non-finite values.
Results may differ from the reference program's by a relative error of at most 0.0031.
Values may be sent and summed in bfloat16 or wider, within the bound.
No kernel may reach another device: no remote copies, remote signals or barrier semaphores. Data moves between devices by JAX's collectives and lax.ppermute only.
A program may use at most 64 MiB of HBM per device.

```python
import jax
import jax.numpy as jnp

PANEL = 512
TRAIL_ROWS = 16384
TRAIL_COLS = 6144


def place_value(shuffled, value, slot):
    where_now = jnp.argmax(shuffled == value)
    taken = shuffled[slot]
    shuffled = shuffled.at[where_now].set(taken)
    return shuffled.at[slot].set(value)


def draw_sources(key, part):
    key = jax.random.fold_in(key, 7)
    first, second, third = jax.random.split(key, 3)
    shuffled = jax.random.permutation(first, TRAIL_ROWS).astype(jnp.int32)
    slot_one = jax.random.randint(second, (), 0, PANEL)
    slot_two = (slot_one + 1 + jax.random.randint(third, (), 0, PANEL - 1)) % PANEL
    shuffled = place_value(shuffled, TRAIL_ROWS - 1, slot_one)
    shuffled = place_value(shuffled, TRAIL_ROWS // 2, slot_two)
    return shuffled[:PANEL].astype(jnp.int32)


def level_of(stream_key, dims, cuts, least, largest):
    def one(axis_at, blocks):
        heights = jax.random.uniform(jax.random.fold_in(jax.random.fold_in(stream_key, 6), axis_at), (blocks,), jnp.float32, least / len(cuts), largest / len(cuts))
        return jnp.repeat(jnp.exp(heights), dims[axis_at] // blocks).reshape((-1,) + (1,) * (len(dims) - axis_at - 1))

    factor_of = one(*cuts[0])
    for cut in cuts[1:]:
        factor_of = factor_of * one(*cut)
    return factor_of


def bell_draw(key, dims, scale, limit, shards=(), kind=jnp.bfloat16):
    result = jax.random.normal(key, dims, jnp.float32) * scale
    if len(shards) > 0:
        result = level_of(key, dims, shards, -0.22, 0.18) * result
    return jnp.clip(result, min=-limit, max=limit).astype(kind)


def setup_inputs(seed: int = 0) -> dict:
    arg_keys = jax.random.split(jax.random.key(seed), 4)
    matrix = bell_draw(arg_keys[0], (TRAIL_ROWS, TRAIL_COLS), 1.0, 6.0, ((0, 32), (1, 16)), jnp.float32)
    panel = bell_draw(arg_keys[1], (TRAIL_ROWS, PANEL), PANEL ** -0.5, 0.25, ((0, 32), (1, 16)), jnp.float32)
    sources = draw_sources(jax.random.fold_in(arg_keys[3], 71), 0)
    return {"matrix": matrix, "panel": panel, "sources": sources}


def assignment(sources):
    width = sources.shape[0]
    top = jnp.arange(width, dtype=jnp.int32)
    used = jnp.any(sources[None, :] == top[:, None], axis=1)
    free_rank = jnp.cumsum(jnp.where(used, 0, 1).astype(jnp.int32)).astype(jnp.int32) - 1
    vacated = sources >= width
    vac_rank = jnp.cumsum(vacated.astype(jnp.int32)).astype(jnp.int32) - 1
    match = jnp.logical_and(jnp.logical_not(used)[None, :], free_rank[None, :] == vac_rank[:, None])
    match = jnp.logical_and(match, vacated[:, None])
    fill = jnp.sum(jnp.where(match, top[None, :], 0), axis=1).astype(jnp.int32)
    return (vacated, fill)

def reference(matrix, panel, sources):
    width = PANEL
    vacated, fill = assignment(sources)
    order = jnp.arange(TRAIL_ROWS, dtype=jnp.int32)
    target = jnp.where(vacated, sources, TRAIL_ROWS).astype(jnp.int32)
    order = order.at[target].set(fill, mode='drop')
    order = order.at[:width].set(sources)
    swapped = jnp.take(matrix, order, axis=0)
    lower = jnp.tril(panel[:width], -1) + jnp.eye(width, dtype=jnp.float32)
    upper = jax.scipy.linalg.solve_triangular(lower, swapped[:width], lower=True, unit_diagonal=True)
    upper_half = upper.astype(jnp.bfloat16)
    multipliers = panel[width:].astype(jnp.bfloat16)
    product = jnp.dot(multipliers.astype(jnp.float32), upper_half.astype(jnp.float32), preferred_element_type=jnp.float32)
    return jnp.concatenate([upper, swapped[width:] - product], axis=0)
```

```python
import jax
import jax.numpy as jnp
from jax import lax
from jax.experimental import pallas as pl
from jax.experimental.pallas import tpu as pltpu
from jax.sharding import Mesh, PartitionSpec as P

GRID_ROW = ("z", "x")
SCALE = 65536.0
VMEM_LIMIT = 48 * 1024 * 1024
HALF = jnp.bfloat16


def call(kernel, out_shape, flops, moved):
    return pl.pallas_call(
        kernel,
        out_shape=out_shape,
        compiler_params=pltpu.CompilerParams(vmem_limit_bytes=VMEM_LIMIT),
        cost_estimate=pl.CostEstimate(flops=flops, bytes_accessed=moved, transcendentals=0),
    )


def grid_row():
    return lax.axis_index("z") * lax.axis_size("x") + lax.axis_index("x")


def exact_dot(left, right):
    return jnp.dot(left, right, precision=lax.Precision.HIGHEST, preferred_element_type=jnp.float32)


def half_dot(left, right):
    return jnp.dot(left, right, preferred_element_type=jnp.float32)


def iota(shape, dim):
    return lax.broadcasted_iota(jnp.int32, shape, dim)


def as_column(row):
    return jnp.transpose(jnp.broadcast_to(row, (8, row.shape[1])))[:, 0:1]


def one_hot(hit):
    return jnp.where(hit, 1.0, 0.0).astype(HALF)


def offer_kernel(row_ref, sources_ref, matrix_ref, columns_ref, out_ref):
    rows, cols = matrix_ref.shape
    width = sources_ref.shape[1]
    parts, each, wide = out_ref.shape
    myself = row_ref[0, 0]

    @pl.when(myself == 0)
    def _():
        out_ref[:, :, 0:cols] = matrix_ref[...].astype(HALF).reshape(parts, each, cols)

    @pl.when(myself != 0)
    def _():
        wanted = as_column(sources_ref[...]) - myself * rows
        picks = one_hot(wanted == iota((width, rows), 1))
        found = half_dot(picks, matrix_ref[...].astype(HALF))
        out_ref[:, :, 0:cols] = found.astype(HALF).reshape(parts, each, cols)

    columns = columns_ref[...]
    first = columns.astype(HALF).astype(jnp.float32)
    rest = columns - first
    second = rest.astype(HALF).astype(jnp.float32)
    third = rest - second
    for part in range(parts):
        high, lane = 4 * (part // 4), 128 * (part % 4)
        pieces = [x[high : high + 4, lane : lane + 128] for x in (first, second, third)]
        piece = jnp.concatenate(pieces + [jnp.zeros((4, 128), jnp.float32)], axis=0)
        out_ref[part, :, cols:wide] = piece.astype(HALF)


def collect_kernel(got_ref, out_ref):
    parts, each, twice = out_ref.shape
    cols = twice // 2
    total = got_ref[1, :, 0:cols].astype(jnp.float32)
    for part in range(2, parts):
        total = total + got_ref[part, :, 0:cols].astype(jnp.float32)
    pivots = total.astype(HALF)
    top = got_ref[0, :, 0:cols]
    for part in range(parts):
        out_ref[part, :, 0:cols] = pivots
        out_ref[part, :, cols:twice] = top


def slices_kernel(pieces_ref, columns_ref, out_ref):
    for part in range(32):
        high, lane = 4 * (part // 4), 128 * (part % 4)
        out_ref[high : high + 4, lane : lane + 128] = pieces_ref[part] * SCALE
    out_ref[32:64, :] = columns_ref[...].astype(HALF).astype(jnp.float32) * SCALE


def invert_block(lower):
    n = lower.shape[0]
    row, col = iota((n, n), 0), iota((n, n), 1)
    unit = jnp.where(row == col, 1.0, 0.0)
    power = jnp.where((row // 32 == col // 32) & (row > col), lower, 0.0)
    inverse = unit - power
    for _ in range(4):
        power = exact_dot(power, power)
        inverse = inverse + exact_dot(inverse, power)
    size = 32
    while size < n:
        off = (row // (2 * size) == col // (2 * size)) & (row // size > col // size)
        below = jnp.where(off, lower, 0.0)
        inverse = inverse - exact_dot(inverse, exact_dot(below, inverse))
        size *= 2
    return inverse


def prepare_kernel(row_ref, core_ref, sources_ref, mine_ref, other_ref, lower_ref, inverse_ref, weights_ref, choose_ref):
    width = sources_ref.shape[1]
    myself = row_ref[0, 0]
    core = core_ref[0, 0]
    chips = mine_ref.shape[0]
    sources = sources_ref[...]
    mine, other = mine_ref[...], other_ref[...]
    even = jnp.where(core == 0, mine, other)
    odd = jnp.where(core == 0, other, mine)
    blocks = []
    for chip in range(chips):
        blocks += [even[chip], odd[chip]]
    spread = jnp.concatenate([b[0:32] for b in blocks], axis=0) * (1.0 / SCALE)
    lower_ref[...] = jnp.transpose(spread)
    multipliers = jnp.concatenate([b[32:64] for b in blocks], axis=0) * (-1.0 / SCALE)
    weights_ref[:, width : 2 * width] = jnp.transpose(multipliers).astype(HALF)
    rows = weights_ref.shape[0]
    weights_ref[:, 0:width] = one_hot(sources - myself * rows == iota((rows, width), 0))

    for block in range(width // 128):
        here = slice(128 * block, 128 * block + 128)
        inverse_ref[here, :] = invert_block(lower_ref[here, here])

    sources_column = as_column(sources)
    square = (width, width)
    chosen = one_hot(sources_column == iota(square, 1))
    choose_ref[0:width, :] = chosen
    used = half_dot(jnp.ones((8, width), HALF), chosen)
    before = one_hot(iota(square, 0) <= iota(square, 1))
    free = 1.0 - used
    free_rank = half_dot(free.astype(HALF), before)
    vacated = jnp.broadcast_to(jnp.where(sources >= width, 1.0, 0.0), (8, width))
    vacated_rank = half_dot(vacated.astype(HALF), before)
    rank_column = jnp.transpose(vacated_rank)[:, 0:1]
    match = (free_rank[0:1] == rank_column) & (free[0:1] > 0.5) & (sources_column >= width)
    choose_ref[width : 2 * width, :] = one_hot(match)


def finish_kernel(row_ref, got_ref, matrix_ref, lower_ref, inverse_ref, weights_ref, choose_ref, out_ref):
    rows, cols = matrix_ref.shape
    width = lower_ref.shape[0]
    top = got_ref[:, :, cols : 2 * cols].reshape(width, cols)
    moved = half_dot(choose_ref[...], top)
    pivots = got_ref[:, :, 0:cols].reshape(width, cols).astype(jnp.float32) + moved[0:width]
    upper = []
    for block in range(width // 128):
        here = slice(128 * block, 128 * block + 128)
        right = pivots[here]
        if block:
            right = right - exact_dot(lower_ref[here, 0 : 128 * block], jnp.concatenate(upper, axis=0))
        upper.append(exact_dot(inverse_ref[here, :], right))
    upper = jnp.concatenate(upper, axis=0)
    myself = row_ref[0, 0]

    @pl.when(myself == 0)
    def _():
        out_ref[...] = upper

    @pl.when(myself != 0)
    def _():
        values = jnp.concatenate([moved[width : 2 * width].astype(HALF), upper.astype(HALF)], axis=0)
        landed = half_dot(weights_ref[:, 0:width], jnp.ones((width, 128), HALF))
        landed = jnp.concatenate([landed] * (cols // 128), axis=1)
        kept = jnp.where(landed > 0.5, 0.0, matrix_ref[...])
        out_ref[...] = kept + half_dot(weights_ref[...], values)


def everyone(block, count):
    return jnp.broadcast_to(block[None], (count,) + block.shape)


def exchange(blocks, axes):
    return lax.all_to_all(blocks, axes, 0, 0, tiled=False)


def on_device(matrix, panel, sources):
    rows, cols = matrix.shape
    width = sources.shape[0]
    parts = lax.axis_size(GRID_ROW)
    chips = lax.axis_size("y")
    each = width // parts
    f32 = jnp.float32
    row = grid_row().reshape(1, 1).astype(jnp.int32)
    core = lax.axis_index("core").reshape(1, 1).astype(jnp.int32)
    sources = sources.reshape(1, width)
    columns = panel.T

    offer = call(
        offer_kernel, jax.ShapeDtypeStruct((parts, each, cols + 128), HALF), 2 * width * rows * cols, 2 * rows * cols * 4
    )(row, sources, matrix, columns)
    got = exchange(offer, GRID_ROW)

    pieces = got[0, :, cols:].astype(f32)
    pieces = pieces[0:4] + pieces[4:8] + pieces[8:12]
    pieces = exchange(everyone(pieces, parts), GRID_ROW)
    slices = call(slices_kernel, jax.ShapeDtypeStruct((64, width), f32), 0, 4 * 64 * width)(pieces, columns)
    mine = exchange(everyone(slices.astype(jnp.float16), chips), "y")
    other = lax.ppermute(mine, "core", [(0, 1), (1, 0)])

    collected = call(
        collect_kernel, jax.ShapeDtypeStruct((parts, each, 2 * cols), HALF), parts * each * cols, 4 * parts * each * cols
    )(got)
    collected, _ = lax.optimization_barrier((collected, mine))
    arrived = exchange(collected, GRID_ROW)

    lower, inverse, weights, choose = call(
        prepare_kernel,
        (
            jax.ShapeDtypeStruct((width, width), f32),
            jax.ShapeDtypeStruct((width, 128), f32),
            jax.ShapeDtypeStruct((rows, 2 * width), HALF),
            jax.ShapeDtypeStruct((2 * width, width), HALF),
        ),
        10 * width * width * width,
        8 * width * width * 4,
    )(row, core, sources, mine.astype(f32), other.astype(f32))
    return call(finish_kernel, jax.ShapeDtypeStruct((rows, cols), f32), 8 * rows * cols * width, 12 * rows * cols * 4)(
        row, arrived, matrix, lower, inverse, weights, choose
    )


def solution(mesh):
    shape = mesh.devices.shape
    chips = mesh.devices.reshape(shape[0] // 8, 8, shape[1] // 2, 2)
    grid = Mesh(chips, ("z", "x", "y", "core"))
    spec = P(GRID_ROW, ("y", "core"))
    return jax.shard_map(on_device, mesh=grid, in_specs=(spec, spec, P()), out_specs=spec, check_vma=False)
```

```python
import jax
import jax.numpy as jnp
from jax import lax
from jax.experimental import pallas as pl
from jax.experimental.pallas import tpu as pltpu
from jax.sharding import Mesh, PartitionSpec as P

GRID_ROW = ("z", "x")
SCALE = 65536.0
ARRIVALS = (0, 4, 1, 5, 2, 6, 7, 3)
VMEM_LIMIT = 20 * 1024 * 1024
VMEM_MOST = 60 * 1024 * 1024
HALF = jnp.bfloat16


def call(kernel, out_shape, flops, moved, limit=VMEM_LIMIT, **more):
    return pl.pallas_call(
        kernel,
        out_shape=out_shape,
        **more,
        compiler_params=pltpu.CompilerParams(vmem_limit_bytes=limit),
        cost_estimate=pl.CostEstimate(flops=flops, bytes_accessed=moved, transcendentals=0),
    )


def grid_row():
    return lax.axis_index("z") * lax.axis_size("x") + lax.axis_index("x")


def exact_dot(left, right):
    return jnp.dot(left, right, precision=lax.Precision.HIGHEST, preferred_element_type=jnp.float32)


def half_dot(left, right):
    return jnp.dot(left, right, preferred_element_type=jnp.float32)


def in_two(values):
    high = values.astype(HALF)
    low = (values - high.astype(jnp.float32)).astype(HALF)
    return jnp.stack([high, low])


def split_dot(left, right):
    high = right.astype(HALF)
    low = (right - high.astype(jnp.float32)).astype(HALF)
    sides = jnp.concatenate([left[0], left[1], left[0]], axis=1)
    return half_dot(sides, jnp.concatenate([high, high, low], axis=0))


def iota(shape, dim):
    return lax.broadcasted_iota(jnp.int32, shape, dim)


def as_column(row):
    return jnp.transpose(jnp.broadcast_to(row, (8, row.shape[1])))[:, 0:1]


def one_hot(hit):
    return jnp.where(hit, 1.0, 0.0).astype(HALF)


def offer_kernel(
    place_ref, sources_hbm, matrix_hbm, columns_hbm, out_hbm, own_ref, sources_ref, matrix_ref, columns_ref, out_ref, sems, sent
):
    rows, cols = matrix_ref.shape
    width = sources_ref.shape[1]
    parts, each, wide = out_ref.shape
    myself = place_ref[0, 0]
    quarter, some = rows // 4, parts // 4
    small = [
        pltpu.make_async_copy(sources_hbm, sources_ref, sems.at[0]),
        pltpu.make_async_copy(columns_hbm, columns_ref, sems.at[1]),
    ]
    large = []
    for at in range(4):
        here = pl.ds(at * quarter, quarter)
        large.append(pltpu.make_async_copy(matrix_hbm.at[here], matrix_ref.at[here], sems.at[2 + at]))
    for copy in small + large:
        copy.start()
    for copy in small:
        copy.wait()

    columns = columns_ref[...]
    own_ref[...] = columns.astype(HALF)
    first = columns.astype(HALF).astype(jnp.float32)
    second = columns - first
    holders = columns.shape[0] // 4
    for part in range(parts):
        high = 4 * (part % holders)
        for piece, lane in ((first, cols), (second, cols + 128)):
            piece = jnp.concatenate([piece[high : high + 4, 128 * q : 128 * q + 128] for q in range(4)], axis=0)
            out_ref[part, :, lane : lane + 128] = piece.astype(HALF)

    def send(at):
        here = pl.ds(at * some, some)
        return pltpu.make_async_copy(out_ref.at[here], out_hbm.at[here], sent.at[at])

    @pl.when(myself == 0)
    def _():
        for at in range(4):
            large[at].wait()
            block = matrix_ref[quarter * at : quarter * (at + 1)].astype(HALF)
            out_ref[some * at : some * (at + 1), :, 0:cols] = block.reshape(some, each, cols)
            send(at).start()

    @pl.when(myself != 0)
    def _():
        wanted = as_column(sources_ref[...]) - myself * rows
        picks = one_hot(wanted == iota((width, rows), 1))
        for copy in large:
            copy.wait()
        block = matrix_ref[...].astype(HALF)
        for at in range(4):
            found = half_dot(picks[quarter * at : quarter * (at + 1)], block).astype(HALF)
            out_ref[some * at : some * (at + 1), :, 0:cols] = found.reshape(some, each, cols)
            send(at).start()

    for at in range(4):
        send(at).wait()


def collect_kernel(got_ref, out_ref):
    parts, each, twice = out_ref.shape
    cols = twice // 2
    total = got_ref[1, :, 0:cols].astype(jnp.float32)
    for part in range(2, parts):
        total = total + got_ref[part, :, 0:cols].astype(jnp.float32)
    pivots = total.astype(HALF)
    top = got_ref[0, :, 0:cols]
    for part in range(parts):
        out_ref[part, :, 0:cols] = pivots
        out_ref[part, :, cols:twice] = top


def invert_block(lower):
    n = lower.shape[0]
    row, col = iota((n, n), 0), iota((n, n), 1)
    unit = jnp.where(row == col, 1.0, 0.0)
    power = jnp.where((row // 32 == col // 32) & (row > col), lower, 0.0)
    inverse = unit - power
    for _ in range(4):
        power = exact_dot(power, power)
        inverse = inverse + exact_dot(inverse, power)
    size = 32
    while size < n:
        off = (row // (2 * size) == col // (2 * size)) & (row // size > col // size)
        below = jnp.where(off, lower, 0.0)
        inverse = inverse - exact_dot(inverse, exact_dot(below, inverse))
        size *= 2
    return inverse


def prepare_kernel(
    place_ref,
    sources_ref,
    mine_ref,
    other_ref,
    own_ref,
    across_ref,
    matrix_ref,
    below_ref,
    inverse_ref,
    weights_ref,
    choose_ref,
    kept_ref,
    lower_ref,
    gathered_ref,
):
    width = sources_ref.shape[1]
    core, chip = place_ref[0, 1], place_ref[0, 2]
    sources = sources_ref[...]
    mine, other = mine_ref[...], other_ref[...]
    pair = (jnp.where(core == 0, mine, other), jnp.where(core == 0, other, mine))
    lines = []
    for at in range(8):
        for half in pair:
            lanes = []
            for q in range(4):
                lanes.append(jnp.concatenate([half[8 * x + at, 4 * q : 4 * q + 4] for x in range(8)], axis=0))
            lines.append(jnp.concatenate(lanes, axis=1))
    lower_ref[...] = jnp.transpose(jnp.concatenate(lines, axis=0)) * (1.0 / SCALE)

    for at, ahead in enumerate(ARRIVALS):
        start = 64 * lax.rem(chip + ahead, 8)
        here = slice(32 * at, 32 * at + 32)
        gathered_ref[pl.ds(pl.multiple_of(start + 32 * core, 32), 32), :] = own_ref[here, :]
        gathered_ref[pl.ds(pl.multiple_of(start + 32 * (1 - core), 32), 32), :] = across_ref[here, :]
    weights_ref[...] = -jnp.transpose(gathered_ref[...])
    rows, cols = matrix_ref.shape
    lands = one_hot(sources - place_ref[0, 0] * rows == iota((rows, width), 0))
    landed = half_dot(lands, jnp.ones((width, 128), HALF))
    kept_ref[...] = jnp.where(jnp.concatenate([landed] * (cols // 128), axis=1) > 0.5, 0.0, matrix_ref[...])

    count = width // 128
    for block in range(count):
        here = slice(128 * block, 128 * block + 128)
        inverse_ref[:, block] = in_two(invert_block(lower_ref[here, here]))
        for at in range(block):
            below_ref[:, block * (block - 1) // 2 + at] = in_two(lower_ref[here, 128 * at : 128 * at + 128])

    sources_column = as_column(sources)
    square = (width, width)
    chosen = one_hot(sources_column == iota(square, 1))
    used = half_dot(jnp.ones((8, width), HALF), chosen)
    before = one_hot(iota(square, 0) <= iota(square, 1))
    free = 1.0 - used
    free_rank = half_dot(free.astype(HALF), before)
    vacated = jnp.broadcast_to(jnp.where(sources >= width, 1.0, 0.0), (8, width))
    vacated_rank = half_dot(vacated.astype(HALF), before)
    rank_column = jnp.transpose(vacated_rank)[:, 0:1]
    match = (free_rank[0:1] == rank_column) & (free[0:1] > 0.5) & (sources_column >= width)
    choose_ref[...] = chosen + one_hot(match)


def finish_kernel(
    place_ref, sources_ref, got_ref, kept_ref, below_ref, inverse_ref, weights_ref, choose_ref, out_hbm, out_ref, sems
):
    rows, cols = kept_ref.shape
    width = sources_ref.shape[1]
    myself = place_ref[0, 0]
    sources = sources_ref[...]
    moved = half_dot(choose_ref[...], got_ref[:, :, cols : 2 * cols].reshape(width, cols))
    found = got_ref[:, :, 0:cols].reshape(width, cols).astype(jnp.float32)
    pivots = jnp.where(as_column(sources) >= width, found, moved)
    upper = []
    for block in range(width // 128):
        here = slice(128 * block, 128 * block + 128)
        right = pivots[here]
        for at in range(block):
            right = right - split_dot(below_ref[:, block * (block - 1) // 2 + at], upper[at])
        upper.append(split_dot(inverse_ref[:, block], right))
    upper = jnp.concatenate(upper, axis=0)

    quarter = rows // 4
    copies = []
    for at in range(4):
        here = pl.ds(at * quarter, quarter)
        copies.append(pltpu.make_async_copy(out_ref.at[here], out_hbm.at[here], sems.at[at]))

    @pl.when(myself == 0)
    def _():
        for at in range(4):
            here = slice(at * quarter, at * quarter + quarter)
            out_ref[here, :] = upper[here]
            copies[at].start()

    @pl.when(myself != 0)
    def _():
        fills, half = moved.astype(HALF), upper.astype(HALF)
        for at in range(4):
            here = slice(at * quarter, at * quarter + quarter)
            lands = one_hot(sources - (myself * rows + at * quarter) == iota((quarter, width), 0))
            change = half_dot(lands, fills) + half_dot(weights_ref[here, :], half)
            out_ref[here, :] = kept_ref[here, :] + change
            copies[at].start()

    for copy in copies:
        copy.wait()


def everyone(block, count):
    return jnp.broadcast_to(block[None], (count,) + block.shape)


def exchange(blocks, axes):
    return lax.all_to_all(blocks, axes, 0, 0, tiled=False)


def on_device(matrix, panel, sources):
    rows, cols = matrix.shape
    width = sources.shape[0]
    parts = lax.axis_size(GRID_ROW)
    chips = lax.axis_size("y")
    each = width // parts
    f32 = jnp.float32
    row = grid_row().astype(jnp.int32)
    place = jnp.stack([row, lax.axis_index("core"), lax.axis_index("y")]).reshape(1, 3).astype(jnp.int32)
    sources = sources.reshape(1, width)
    columns = panel.T
    smem, vmem = pl.BlockSpec(memory_space=pltpu.SMEM), pl.BlockSpec(memory_space=pltpu.VMEM)
    hbm = pl.BlockSpec(memory_space=pltpu.HBM)

    offer, own = call(
        offer_kernel,
        (jax.ShapeDtypeStruct((parts, each, cols + 256), HALF), jax.ShapeDtypeStruct(columns.shape, HALF)),
        2 * width * rows * cols,
        2 * rows * cols * 4,
        limit=VMEM_MOST,
        in_specs=[smem, hbm, hbm, hbm],
        out_specs=[hbm, vmem],
        scratch_shapes=[
            pltpu.VMEM((1, width), jnp.int32),
            pltpu.VMEM((rows, cols), f32),
            pltpu.VMEM(columns.shape, f32),
            pltpu.VMEM((parts, each, cols + 256), HALF),
            pltpu.SemaphoreType.DMA((6,)),
            pltpu.SemaphoreType.DMA((4,)),
        ],
    )(place, sources, matrix, columns)
    got = exchange(offer, GRID_ROW)

    def bring(block, ahead):
        return lax.ppermute(block, "y", [(i, (i - ahead) % chips) for i in range(chips)])

    own = jnp.concatenate([own, bring(own, 4)], axis=0)
    came = [bring(own, 1), bring(own, 2), bring(own, 7)]

    piece = got[0, :, cols : cols + 128].astype(f32) + got[0, :, cols + 128 : cols + 256].astype(f32)
    piece = (piece * SCALE).astype(jnp.float16)
    piece, own, came[0], came[1] = lax.optimization_barrier((piece, own, came[0], came[1]))
    mine = exchange(everyone(piece, 8 * chips), ("x", "y"))

    collected = call(
        collect_kernel, jax.ShapeDtypeStruct((parts, each, 2 * cols), HALF), parts * each * cols, 4 * parts * each * cols
    )(got)
    own = jnp.concatenate([own] + came, axis=0)
    collected, mine, own = lax.optimization_barrier((collected, mine, own))
    arrived = exchange(collected, GRID_ROW)
    other = lax.ppermute(mine, "core", [(0, 1), (1, 0)])
    across = lax.ppermute(own, "core", [(0, 1), (1, 0)])

    below, inverse, weights, choose, kept = call(
        prepare_kernel,
        (
            jax.ShapeDtypeStruct((2, 6, 128, 128), HALF),
            jax.ShapeDtypeStruct((2, 4, 128, 128), HALF),
            jax.ShapeDtypeStruct((rows, width), HALF),
            jax.ShapeDtypeStruct((width, width), HALF),
            jax.ShapeDtypeStruct((rows, cols), f32),
        ),
        10 * width * width * width,
        8 * width * width * 4,
        in_specs=[smem] + [vmem] * 6,
        scratch_shapes=[pltpu.VMEM((width, width), f32), pltpu.VMEM((width, rows), HALF)],
    )(place, sources, mine.astype(f32), other.astype(f32), own, across, matrix)
    return call(
        finish_kernel,
        jax.ShapeDtypeStruct((rows, cols), f32),
        8 * rows * cols * width,
        12 * rows * cols * 4,
        in_specs=[smem] + [vmem] * 7,
        out_specs=hbm,
        scratch_shapes=[pltpu.VMEM((rows, cols), f32), pltpu.SemaphoreType.DMA((4,))],
    )(place, sources, arrived, kept, below, inverse, weights, choose)


def solution(mesh):
    shape = mesh.devices.shape
    chips = mesh.devices.reshape(shape[0] // 8, 8, shape[1] // 2, 2)
    grid = Mesh(chips, ("z", "x", "y", "core"))
    spec = P(GRID_ROW, ("y", "core"))
    return jax.shard_map(on_device, mesh=grid, in_specs=(spec, spec, P()), out_specs=spec, check_vma=False)
```

```python
import jax
import jax.numpy as jnp
from jax import lax
from jax.experimental import pallas as pl
from jax.experimental.pallas import tpu as pltpu
from jax.sharding import Mesh, PartitionSpec as P

GRID_ROW = ("z", "x")
SCALE = 65536.0
ARRIVALS = (0, 4, 2, 6, 1, 5, 3, 7)
VMEM_LIMIT = 20 * 1024 * 1024
VMEM_MOST = 60 * 1024 * 1024
HALF = jnp.bfloat16


def call(kernel, out_shape, flops, moved, limit=VMEM_LIMIT, **more):
    return pl.pallas_call(
        kernel,
        out_shape=out_shape,
        **more,
        compiler_params=pltpu.CompilerParams(vmem_limit_bytes=limit),
        cost_estimate=pl.CostEstimate(flops=flops, bytes_accessed=moved, transcendentals=0),
    )


def grid_row():
    return lax.axis_index("z") * lax.axis_size("x") + lax.axis_index("x")


def exact_dot(left, right):
    return jnp.dot(left, right, precision=lax.Precision.HIGHEST, preferred_element_type=jnp.float32)


def half_dot(left, right):
    return jnp.dot(left, right, preferred_element_type=jnp.float32)


def in_two(values):
    high = values.astype(HALF)
    low = (values - high.astype(jnp.float32)).astype(HALF)
    return jnp.stack([high, low])


def split_dot(left, right):
    high = right.astype(HALF)
    low = (right - high.astype(jnp.float32)).astype(HALF)
    sides = jnp.concatenate([left[0], left[1], left[0]], axis=1)
    return half_dot(sides, jnp.concatenate([high, high, low], axis=0))


def iota(shape, dim):
    return lax.broadcasted_iota(jnp.int32, shape, dim)


def as_column(row):
    return jnp.transpose(jnp.broadcast_to(row, (8, row.shape[1])))[:, 0:1]


def one_hot(hit):
    return jnp.where(hit, 1.0, 0.0).astype(HALF)


def offer_kernel(
    sources_hbm, matrix_hbm, columns_hbm, out_hbm, own_ref, sources_ref, matrix_ref, columns_ref, out_ref, sems, sent
):
    rows, cols = matrix_ref.shape
    width = sources_ref.shape[1]
    parts, each, wide = out_ref.shape
    myself = grid_row()
    quarter, some = rows // 4, parts // 4
    small = [
        pltpu.make_async_copy(sources_hbm, sources_ref, sems.at[0]),
        pltpu.make_async_copy(columns_hbm, columns_ref, sems.at[1]),
    ]
    large = []
    for at in range(4):
        here = pl.ds(at * quarter, quarter)
        large.append(pltpu.make_async_copy(matrix_hbm.at[here], matrix_ref.at[here], sems.at[2 + at]))
    for copy in small + large:
        copy.start()
    for copy in small:
        copy.wait()

    columns = columns_ref[...]
    own_ref[...] = columns.astype(HALF)
    first = columns.astype(HALF).astype(jnp.float32)
    second = columns - first
    holders = columns.shape[0] // 4
    for holder in range(holders):
        high = 4 * holder
        for values, lane in ((first, cols), (second, cols + 128)):
            piece = jnp.concatenate([values[high : high + 4, 128 * q : 128 * q + 128] for q in range(4)], axis=0)
            piece = piece.astype(HALF)
            for part in range(holder, parts, holders):
                out_ref[part, :, lane : lane + 128] = piece

    def send(at):
        here = pl.ds(at * some, some)
        return pltpu.make_async_copy(out_ref.at[here], out_hbm.at[here], sent.at[at])

    @pl.when(myself == 0)
    def _():
        for at in range(4):
            large[at].wait()
            block = matrix_ref[quarter * at : quarter * (at + 1)].astype(HALF)
            out_ref[some * at : some * (at + 1), :, 0:cols] = block.reshape(some, each, cols)
            send(at).start()

    @pl.when(myself != 0)
    def _():
        wanted = as_column(sources_ref[...]) - myself * rows
        picks = one_hot(wanted == iota((width, rows), 1))
        for copy in large:
            copy.wait()
        block = matrix_ref[...].astype(HALF)
        for at in range(4):
            found = half_dot(picks[quarter * at : quarter * (at + 1)], block).astype(HALF)
            out_ref[some * at : some * (at + 1), :, 0:cols] = found.reshape(some, each, cols)
            send(at).start()

    for at in range(4):
        send(at).wait()


def collect_kernel(got_ref, out_ref):
    parts, each, twice = out_ref.shape
    cols = twice // 2
    total = got_ref[1, :, 0:cols].astype(jnp.float32)
    for part in range(2, parts):
        total = total + got_ref[part, :, 0:cols].astype(jnp.float32)
    pivots = total.astype(HALF)
    top = got_ref[0, :, 0:cols]
    for part in range(parts):
        out_ref[part, :, 0:cols] = pivots
        out_ref[part, :, cols:twice] = top


def invert_block(lower):
    n = lower.shape[0]
    row, col = iota((n, n), 0), iota((n, n), 1)
    unit = jnp.where(row == col, 1.0, 0.0)
    power = jnp.where((row // 32 == col // 32) & (row > col), lower, 0.0)
    inverse = unit - power
    for _ in range(4):
        power = exact_dot(power, power)
        inverse = inverse + exact_dot(inverse, power)
    size = 32
    while size < n:
        off = (row // (2 * size) == col // (2 * size)) & (row // size > col // size)
        below = jnp.where(off, lower, 0.0)
        inverse = inverse - exact_dot(inverse, exact_dot(below, inverse))
        size *= 2
    return inverse


def prepare_kernel(
    mine_ref,
    other_ref,
    own_ref,
    across_ref,
    below_ref,
    inverse_ref,
    weights_ref,
    lower_ref,
    gathered_ref,
):
    width = lower_ref.shape[0]
    core, chip = lax.axis_index("core"), lax.axis_index("y")
    mine, other = mine_ref[...], other_ref[...]
    pair = (jnp.where(core == 0, mine, other), jnp.where(core == 0, other, mine))
    lines = []
    for at in range(8):
        for half in pair:
            lanes = []
            for q in range(4):
                lanes.append(jnp.concatenate([half[8 * x + at, 4 * q : 4 * q + 4] for x in range(8)], axis=0))
            lines.append(jnp.concatenate(lanes, axis=1))
    lower_ref[...] = jnp.transpose(jnp.concatenate(lines, axis=0)) * (1.0 / SCALE)

    for at, ahead in enumerate(ARRIVALS):
        start = 64 * lax.rem(chip + ahead, 8)
        here = slice(32 * at, 32 * at + 32)
        gathered_ref[pl.ds(pl.multiple_of(start + 32 * core, 32), 32), :] = own_ref[here, :]
        gathered_ref[pl.ds(pl.multiple_of(start + 32 * (1 - core), 32), 32), :] = across_ref[here, :]
    weights_ref[...] = -jnp.transpose(gathered_ref[...])

    count = width // 128
    for block in range(count):
        here = slice(128 * block, 128 * block + 128)
        inverse_ref[:, block] = in_two(invert_block(lower_ref[here, here]))
        for at in range(block):
            below_ref[:, block * (block - 1) // 2 + at] = in_two(lower_ref[here, 128 * at : 128 * at + 128])


def choose_kernel(sources_ref, matrix_ref, choose_ref, kept_ref):
    width = sources_ref.shape[1]
    sources = sources_ref[...]
    rows, cols = matrix_ref.shape
    lands = one_hot(sources - grid_row() * rows == iota((rows, width), 0))
    landed = half_dot(lands, jnp.ones((width, 128), HALF))
    kept_ref[...] = jnp.where(jnp.concatenate([landed] * (cols // 128), axis=1) > 0.5, 0.0, matrix_ref[...])

    sources_column = as_column(sources)
    square = (width, width)
    chosen = one_hot(sources_column == iota(square, 1))
    used = half_dot(jnp.ones((8, width), HALF), chosen)
    before = one_hot(iota(square, 0) <= iota(square, 1))
    free = 1.0 - used
    free_rank = half_dot(free.astype(HALF), before)
    vacated = jnp.broadcast_to(jnp.where(sources >= width, 1.0, 0.0), (8, width))
    vacated_rank = half_dot(vacated.astype(HALF), before)
    rank_column = jnp.transpose(vacated_rank)[:, 0:1]
    match = (free_rank[0:1] == rank_column) & (free[0:1] > 0.5) & (sources_column >= width)
    choose_ref[...] = chosen + one_hot(match)


def finish_kernel(
    sources_ref, got_ref, kept_ref, below_ref, inverse_ref, weights_ref, choose_ref, out_hbm, out_ref, sems
):
    rows, cols = kept_ref.shape
    width = sources_ref.shape[1]
    myself = grid_row()
    sources = sources_ref[...]
    moved = half_dot(choose_ref[...], got_ref[:, :, cols : 2 * cols].reshape(width, cols))
    found = got_ref[:, :, 0:cols].reshape(width, cols).astype(jnp.float32)
    pivots = jnp.where(as_column(sources) >= width, found, moved)
    upper = []
    for block in range(width // 128):
        here = slice(128 * block, 128 * block + 128)
        right = pivots[here]
        for at in range(block):
            right = right - split_dot(below_ref[:, block * (block - 1) // 2 + at], upper[at])
        upper.append(split_dot(inverse_ref[:, block], right))
    upper = jnp.concatenate(upper, axis=0)

    quarter = rows // 4
    copies = []
    for at in range(4):
        here = pl.ds(at * quarter, quarter)
        copies.append(pltpu.make_async_copy(out_ref.at[here], out_hbm.at[here], sems.at[at]))

    @pl.when(myself == 0)
    def _():
        for at in range(4):
            here = slice(at * quarter, at * quarter + quarter)
            out_ref[here, :] = upper[here]
            copies[at].start()

    @pl.when(myself != 0)
    def _():
        fills, half = moved.astype(HALF), upper.astype(HALF)
        for at in range(4):
            here = slice(at * quarter, at * quarter + quarter)
            lands = one_hot(sources - (myself * rows + at * quarter) == iota((quarter, width), 0))
            change = half_dot(lands, fills) + half_dot(weights_ref[here, :], half)
            out_ref[here, :] = kept_ref[here, :] + change
            copies[at].start()

    for copy in copies:
        copy.wait()


def everyone(block, count):
    return jnp.broadcast_to(block[None], (count,) + block.shape)


def exchange(blocks, axes):
    return lax.all_to_all(blocks, axes, 0, 0, tiled=False)


def on_device(matrix, panel, sources):
    rows, cols = matrix.shape
    width = sources.shape[0]
    parts = lax.axis_size(GRID_ROW)
    chips = lax.axis_size("y")
    each = width // parts
    f32 = jnp.float32
    sources = sources.reshape(1, width)
    columns = panel.T
    vmem = pl.BlockSpec(memory_space=pltpu.VMEM)
    hbm = pl.BlockSpec(memory_space=pltpu.HBM)

    offer, own = call(
        offer_kernel,
        (jax.ShapeDtypeStruct((parts, each, cols + 256), HALF), jax.ShapeDtypeStruct(columns.shape, HALF)),
        2 * width * rows * cols,
        2 * rows * cols * 4,
        limit=VMEM_MOST,
        in_specs=[hbm, hbm, hbm],
        out_specs=[hbm, vmem],
        scratch_shapes=[
            pltpu.VMEM((1, width), jnp.int32),
            pltpu.VMEM((rows, cols), f32),
            pltpu.VMEM(columns.shape, f32),
            pltpu.VMEM((parts, each, cols + 256), HALF),
            pltpu.SemaphoreType.DMA((6,)),
            pltpu.SemaphoreType.DMA((4,)),
        ],
    )(sources, matrix, columns)
    got = exchange(offer, GRID_ROW)

    choose, kept = call(
        choose_kernel,
        (jax.ShapeDtypeStruct((width, width), HALF), jax.ShapeDtypeStruct((rows, cols), f32)),
        4 * width * width * width,
        4 * rows * cols * 4,
    )(sources, matrix)

    def bring(block, ahead):
        return lax.ppermute(block, "y", [(i, (i - ahead) % chips) for i in range(chips)])

    own = jnp.concatenate([own, bring(own, 4)], axis=0)
    own = jnp.concatenate([own, bring(own, 2)], axis=0)

    piece = got[0, :, cols : cols + 128].astype(f32) + got[0, :, cols + 128 : cols + 256].astype(f32)
    piece = (piece * SCALE).astype(jnp.float16)
    piece, own, choose, kept = lax.optimization_barrier((piece, own, choose, kept))
    mine = exchange(everyone(piece, 8 * chips), ("x", "y"))

    collected = call(
        collect_kernel, jax.ShapeDtypeStruct((parts, each, 2 * cols), HALF), parts * each * cols, 4 * parts * each * cols
    )(got)
    own = jnp.concatenate([own, bring(own, 1)], axis=0)
    collected, mine, own = lax.optimization_barrier((collected, mine, own))
    arrived = exchange(collected, GRID_ROW)
    other = lax.ppermute(mine, "core", [(0, 1), (1, 0)])
    across = lax.ppermute(own, "core", [(0, 1), (1, 0)])

    below, inverse, weights = call(
        prepare_kernel,
        (
            jax.ShapeDtypeStruct((2, 6, 128, 128), HALF),
            jax.ShapeDtypeStruct((2, 4, 128, 128), HALF),
            jax.ShapeDtypeStruct((rows, width), HALF),
        ),
        10 * width * width * width,
        8 * width * width * 4,
        scratch_shapes=[pltpu.VMEM((width, width), f32), pltpu.VMEM((width, rows), HALF)],
    )(mine.astype(f32), other.astype(f32), own, across)
    return call(
        finish_kernel,
        jax.ShapeDtypeStruct((rows, cols), f32),
        8 * rows * cols * width,
        12 * rows * cols * 4,
        in_specs=[vmem] * 7,
        out_specs=hbm,
        scratch_shapes=[pltpu.VMEM((rows, cols), f32), pltpu.SemaphoreType.DMA((4,))],
    )(sources, arrived, kept, below, inverse, weights, choose)


def solution(mesh):
    shape = mesh.devices.shape
    chips = mesh.devices.reshape(shape[0] // 8, 8, shape[1] // 2, 2)
    grid = Mesh(chips, ("z", "x", "y", "core"))
    spec = P(GRID_ROW, ("y", "core"))
    return jax.shard_map(on_device, mesh=grid, in_specs=(spec, spec, P()), out_specs=spec, check_vma=False)
```

```python
import jax
import jax.numpy as jnp
from jax import lax
from jax.experimental import pallas as pl
from jax.experimental.pallas import tpu as pltpu
from jax.sharding import Mesh, PartitionSpec as P

GRID_ROW = ("z", "x")
SCALE = 65536.0
ARRIVALS = (0, 4, 2, 6, 1, 5, 3, 7)
STEPS = ((0, 1, 0), (0, 2, 1), (0, 3, 2), (1, 2, 3), (1, 3, 4), (2, 3, 5))
VMEM_LIMIT = 20 * 1024 * 1024
HALF = jnp.bfloat16


def call(kernel, out_shape, flops, moved, **more):
    return pl.pallas_call(
        kernel,
        out_shape=out_shape,
        **more,
        compiler_params=pltpu.CompilerParams(vmem_limit_bytes=VMEM_LIMIT),
        cost_estimate=pl.CostEstimate(flops=flops, bytes_accessed=moved, transcendentals=0),
    )


def in_hbm(array):
    return pltpu.with_memory_space_constraint(array, pltpu.HBM)


def grid_row():
    return lax.axis_index("z") * lax.axis_size("x") + lax.axis_index("x")


def exact_dot(left, right):
    return jnp.dot(left, right, precision=lax.Precision.HIGHEST, preferred_element_type=jnp.float32)


def half_dot(left, right):
    return jnp.dot(left, right, preferred_element_type=jnp.float32)


def in_two(values):
    high = values.astype(HALF)
    low = (values - high.astype(jnp.float32)).astype(HALF)
    return jnp.stack([high, low])


def split_dot(left, right):
    high = right.astype(HALF)
    low = (right - high.astype(jnp.float32)).astype(HALF)
    sides = jnp.concatenate([left[0], left[1], left[0]], axis=1)
    return half_dot(sides, jnp.concatenate([high, high, low], axis=0))


def iota(shape, dim):
    return lax.broadcasted_iota(jnp.int32, shape, dim)


def as_column(row):
    return jnp.transpose(jnp.broadcast_to(row, (8, row.shape[1])))[:, 0:1]


def one_hot(hit):
    return jnp.where(hit, 1.0, 0.0).astype(HALF)


def offer_kernel(
    sources_hbm, matrix_hbm, columns_hbm, out_hbm, own_ref, sources_ref, matrix_ref, columns_ref, out_ref, sems, sent
):
    rows, cols = matrix_ref.shape
    width = sources_ref.shape[1]
    parts, each, wide = out_ref.shape
    myself = grid_row()
    quarter, some = rows // 4, parts // 4
    small = [
        pltpu.make_async_copy(sources_hbm, sources_ref, sems.at[0]),
        pltpu.make_async_copy(columns_hbm, columns_ref, sems.at[1]),
    ]
    large = []
    for at in range(4):
        here = pl.ds(at * quarter, quarter)
        large.append(pltpu.make_async_copy(matrix_hbm.at[here], matrix_ref.at[here], sems.at[2 + at]))
    for copy in small + large:
        copy.start()
    for copy in small:
        copy.wait()

    columns = columns_ref[...]
    own_ref[...] = columns.astype(HALF)
    first = columns.astype(HALF).astype(jnp.float32)
    second = columns - first
    holders = columns.shape[0] // 4
    for holder in range(holders):
        high = 4 * holder
        for values, lane in ((first, cols), (second, cols + 128)):
            piece = jnp.concatenate([values[high : high + 4, 128 * q : 128 * q + 128] for q in range(4)], axis=0)
            piece = piece.astype(HALF)
            for part in range(holder, parts, holders):
                out_ref[part, :, lane : lane + 128] = piece

    def send(at):
        here = pl.ds(at * some, some)
        return pltpu.make_async_copy(out_ref.at[here], out_hbm.at[here], sent.at[at])

    @pl.when(myself == 0)
    def _():
        for at in range(4):
            large[at].wait()
            block = matrix_ref[quarter * at : quarter * (at + 1)].astype(HALF)
            out_ref[some * at : some * (at + 1), :, 0:cols] = block.reshape(some, each, cols)
            send(at).start()

    @pl.when(myself != 0)
    def _():
        wanted = as_column(sources_ref[...]) - myself * rows
        picks = one_hot(wanted == iota((width, rows), 1))
        for copy in large:
            copy.wait()
        block = matrix_ref[...].astype(HALF)
        for at in range(4):
            found = half_dot(picks[quarter * at : quarter * (at + 1)], block).astype(HALF)
            out_ref[some * at : some * (at + 1), :, 0:cols] = found.reshape(some, each, cols)
            send(at).start()

    for at in range(4):
        send(at).wait()


def collect_kernel(got_ref, out_ref):
    parts, each, twice = out_ref.shape
    cols = twice // 2
    total = got_ref[1, :, 0:cols].astype(jnp.float32)
    for part in range(2, parts):
        total = total + got_ref[part, :, 0:cols].astype(jnp.float32)
    pivots = total.astype(HALF)
    top = got_ref[0, :, 0:cols]
    for part in range(parts):
        out_ref[part, :, 0:cols] = pivots
        out_ref[part, :, cols:twice] = top


def invert_block(lower):
    n = lower.shape[0]
    row, col = iota((n, n), 0), iota((n, n), 1)
    unit = jnp.where(row == col, 1.0, 0.0)
    power = jnp.where((row // 32 == col // 32) & (row > col), lower, 0.0)
    inverse = unit - power
    for _ in range(4):
        power = exact_dot(power, power)
        inverse = inverse + exact_dot(inverse, power)
    size = 32
    while size < n:
        off = (row // (2 * size) == col // (2 * size)) & (row // size > col // size)
        below = jnp.where(off, lower, 0.0)
        inverse = inverse - exact_dot(inverse, exact_dot(below, inverse))
        size *= 2
    return inverse


def prepare_kernel(
    mine_ref,
    other_ref,
    own_ref,
    across_ref,
    below_ref,
    inverse_ref,
    weights_ref,
    lower_ref,
    gathered_ref,
):
    width = lower_ref.shape[0]
    core, chip = lax.axis_index("core"), lax.axis_index("y")
    mine, other = mine_ref[...], other_ref[...]
    pair = (jnp.where(core == 0, mine, other), jnp.where(core == 0, other, mine))
    lines = []
    for at in range(8):
        for half in pair:
            lanes = []
            for q in range(4):
                lanes.append(jnp.concatenate([half[8 * x + at, 4 * q : 4 * q + 4] for x in range(8)], axis=0))
            lines.append(jnp.concatenate(lanes, axis=1))
    lower_ref[...] = jnp.transpose(jnp.concatenate(lines, axis=0)) * (1.0 / SCALE)

    for at, ahead in enumerate(ARRIVALS):
        start = 64 * lax.rem(chip + ahead, 8)
        here = slice(32 * at, 32 * at + 32)
        gathered_ref[pl.ds(pl.multiple_of(start + 32 * core, 32), 32), :] = own_ref[here, :]
        gathered_ref[pl.ds(pl.multiple_of(start + 32 * (1 - core), 32), 32), :] = across_ref[here, :]
    weights_ref[...] = -jnp.transpose(gathered_ref[...])

    count = width // 128
    inverses = []
    for block in range(count):
        here = slice(128 * block, 128 * block + 128)
        inverses.append(invert_block(lower_ref[here, here]))
        inverse_ref[:, block] = in_two(inverses[block])
    for at, block, place in STEPS:
        here = slice(128 * block, 128 * block + 128)
        below_ref[:, place] = in_two(-exact_dot(inverses[block], lower_ref[here, 128 * at : 128 * at + 128]))


def choose_kernel(sources_ref, matrix_ref, choose_ref, kept_ref):
    width = sources_ref.shape[1]
    sources = sources_ref[...]
    rows, cols = matrix_ref.shape
    lands = one_hot(sources - grid_row() * rows == iota((rows, width), 0))
    landed = half_dot(lands, jnp.ones((width, 128), HALF))
    kept_ref[...] = jnp.where(jnp.concatenate([landed] * (cols // 128), axis=1) > 0.5, 0.0, matrix_ref[...])

    sources_column = as_column(sources)
    square = (width, width)
    chosen = one_hot(sources_column == iota(square, 1))
    used = half_dot(jnp.ones((8, width), HALF), chosen)
    before = one_hot(iota(square, 0) <= iota(square, 1))
    free = 1.0 - used
    free_rank = half_dot(free.astype(HALF), before)
    vacated = jnp.broadcast_to(jnp.where(sources >= width, 1.0, 0.0), (8, width))
    vacated_rank = half_dot(vacated.astype(HALF), before)
    rank_column = jnp.transpose(vacated_rank)[:, 0:1]
    match = (free_rank[0:1] == rank_column) & (free[0:1] > 0.5) & (sources_column >= width)
    choose_ref[...] = chosen + one_hot(match)


def finish_kernel(
    sources_ref, got_ref, kept_ref, below_ref, inverse_ref, weights_ref, choose_ref, out_hbm, out_ref, sems
):
    rows, cols = kept_ref.shape
    width = sources_ref.shape[1]
    myself = grid_row()
    sources = sources_ref[...]
    moved = half_dot(choose_ref[...], got_ref[:, :, cols : 2 * cols].reshape(width, cols))
    found = got_ref[:, :, 0:cols].reshape(width, cols).astype(jnp.float32)
    pivots = jnp.where(as_column(sources) >= width, found, moved)
    count = width // 128
    upper = []
    for block in range(count):
        upper.append(split_dot(inverse_ref[:, block], pivots[128 * block : 128 * block + 128]))
    first = 0
    for at in range(count - 1):
        more = count - 1 - at
        change = split_dot(below_ref[:, first : first + more].reshape(2, 128 * more, 128), upper[at])
        for block in range(more):
            upper[at + 1 + block] = upper[at + 1 + block] + change[128 * block : 128 * block + 128]
        first += more
    upper = jnp.concatenate(upper, axis=0)

    quarter = rows // 4
    copies = []
    for at in range(4):
        here = pl.ds(at * quarter, quarter)
        copies.append(pltpu.make_async_copy(out_ref.at[here], out_hbm.at[here], sems.at[at]))

    @pl.when(myself == 0)
    def _():
        for at in range(4):
            here = slice(at * quarter, at * quarter + quarter)
            out_ref[here, :] = upper[here]
            copies[at].start()

    @pl.when(myself != 0)
    def _():
        fills, half = moved.astype(HALF), upper.astype(HALF)
        for at in range(4):
            here = slice(at * quarter, at * quarter + quarter)
            lands = one_hot(sources - (myself * rows + at * quarter) == iota((quarter, width), 0))
            change = half_dot(lands, fills) + half_dot(weights_ref[here, :], half)
            out_ref[here, :] = kept_ref[here, :] + change
            copies[at].start()

    for copy in copies:
        copy.wait()


def everyone(block, count):
    return jnp.broadcast_to(block[None], (count,) + block.shape)


def exchange(blocks, axes):
    return lax.all_to_all(blocks, axes, 0, 0, tiled=False)


def on_device(matrix, panel, sources):
    rows, cols = matrix.shape
    width = sources.shape[0]
    parts = lax.axis_size(GRID_ROW)
    chips = lax.axis_size("y")
    each = width // parts
    f32 = jnp.float32
    sources = sources.reshape(1, width)
    columns = panel.T
    vmem = pl.BlockSpec(memory_space=pltpu.VMEM)
    hbm = pl.BlockSpec(memory_space=pltpu.HBM)

    offer, own = call(
        offer_kernel,
        (jax.ShapeDtypeStruct((parts, each, cols + 256), HALF), jax.ShapeDtypeStruct(columns.shape, HALF)),
        2 * width * rows * cols,
        2 * rows * cols * 4,
        in_specs=[hbm, hbm, hbm],
        out_specs=[hbm, vmem],
        scratch_shapes=[
            pltpu.VMEM((1, width), jnp.int32),
            pltpu.VMEM((rows, cols), f32),
            pltpu.VMEM(columns.shape, f32),
            pltpu.VMEM((parts, each, cols + 256), HALF),
            pltpu.SemaphoreType.DMA((6,)),
            pltpu.SemaphoreType.DMA((4,)),
        ],
    )(in_hbm(sources), in_hbm(matrix), in_hbm(columns))
    got = exchange(offer, GRID_ROW)

    choose, kept = call(
        choose_kernel,
        (jax.ShapeDtypeStruct((width, width), HALF), jax.ShapeDtypeStruct((rows, cols), f32)),
        4 * width * width * width,
        4 * rows * cols * 4,
    )(sources, matrix)

    def bring(block, ahead):
        return lax.ppermute(block, "y", [(i, (i - ahead) % chips) for i in range(chips)])

    own = jnp.concatenate([own, bring(own, 4)], axis=0)
    came = bring(own, 2)

    piece = got[0, :, cols : cols + 128].astype(f32) + got[0, :, cols + 128 : cols + 256].astype(f32)
    piece = (piece * SCALE).astype(jnp.float16)
    piece, came, choose, kept = lax.optimization_barrier((piece, came, choose, kept))
    mine = exchange(everyone(piece, 8 * chips), ("x", "y"))

    collected = call(
        collect_kernel, jax.ShapeDtypeStruct((parts, each, 2 * cols), HALF), parts * each * cols, 4 * parts * each * cols
    )(got)
    own = jnp.concatenate([own, came], axis=0)
    came = bring(own, 1)
    collected, mine, came = lax.optimization_barrier((collected, mine, came))
    own = jnp.concatenate([own, came], axis=0)
    arrived = exchange(collected, GRID_ROW)
    other = lax.ppermute(mine, "core", [(0, 1), (1, 0)])
    across = lax.ppermute(own, "core", [(0, 1), (1, 0)])

    below, inverse, weights = call(
        prepare_kernel,
        (
            jax.ShapeDtypeStruct((2, 6, 128, 128), HALF),
            jax.ShapeDtypeStruct((2, 4, 128, 128), HALF),
            jax.ShapeDtypeStruct((rows, width), HALF),
        ),
        10 * width * width * width,
        8 * width * width * 4,
        scratch_shapes=[pltpu.VMEM((width, width), f32), pltpu.VMEM((width, rows), HALF)],
    )(mine.astype(f32), other.astype(f32), own, across)
    return call(
        finish_kernel,
        jax.ShapeDtypeStruct((rows, cols), f32),
        8 * rows * cols * width,
        12 * rows * cols * 4,
        in_specs=[vmem] * 7,
        out_specs=hbm,
        scratch_shapes=[pltpu.VMEM((rows, cols), f32), pltpu.SemaphoreType.DMA((4,))],
    )(sources, arrived, kept, below, inverse, weights, choose)


def solution(mesh):
    shape = mesh.devices.shape
    chips = mesh.devices.reshape(shape[0] // 8, 8, shape[1] // 2, 2)
    grid = Mesh(chips, ("z", "x", "y", "core"))
    spec = P(GRID_ROW, ("y", "core"))
    return jax.shard_map(on_device, mesh=grid, in_specs=(spec, spec, P()), out_specs=spec, check_vma=False)
```

```python
import jax
import jax.numpy as jnp
from jax import lax
from jax.experimental import pallas as pl
from jax.experimental.pallas import tpu as pltpu
from jax.sharding import Mesh, PartitionSpec as P

GRID_ROW = ("z", "x")
SCALE = 65536.0
ARRIVALS = (0, 4, 2, 1, 5, 3, 6, 7)
STEPS = ((0, 1, 0), (0, 2, 1), (0, 3, 2), (1, 2, 3), (1, 3, 4), (2, 3, 5))
VMEM_LIMIT = 20 * 1024 * 1024
HALF = jnp.bfloat16
SHORT = jnp.float16


def call(kernel, out_shape, flops, moved, **more):
    return pl.pallas_call(
        kernel,
        out_shape=out_shape,
        **more,
        compiler_params=pltpu.CompilerParams(vmem_limit_bytes=VMEM_LIMIT),
        cost_estimate=pl.CostEstimate(flops=flops, bytes_accessed=moved, transcendentals=0),
    )


def in_hbm(array):
    return pltpu.with_memory_space_constraint(array, pltpu.HBM)


def grid_row():
    return lax.axis_index("z") * lax.axis_size("x") + lax.axis_index("x")


def exact_dot(left, right):
    return jnp.dot(left, right, precision=lax.Precision.HIGHEST, preferred_element_type=jnp.float32)


def half_dot(left, right):
    return jnp.dot(left, right, preferred_element_type=jnp.float32)


def in_two(values):
    high = values.astype(HALF)
    low = (values - high.astype(jnp.float32)).astype(HALF)
    return jnp.stack([high, low])


def split_dot(left, right):
    high = right.astype(HALF)
    low = (right - high.astype(jnp.float32)).astype(HALF)
    sides = jnp.concatenate([left[0], left[1], left[0]], axis=1)
    return half_dot(sides, jnp.concatenate([high, high, low], axis=0))


def iota(shape, dim):
    return lax.broadcasted_iota(jnp.int32, shape, dim)


def as_column(row):
    return jnp.transpose(jnp.broadcast_to(row, (8, row.shape[1])))[:, 0:1]


def one_hot(hit):
    return jnp.where(hit, 1.0, 0.0).astype(HALF)


def range_power(block):
    largest = jnp.maximum(jnp.max(jnp.abs(block)), 1e-30)
    return 13.0 - jnp.ceil(jnp.log2(jnp.full((1, 1), largest, jnp.float32)))


def offer_kernel(sources_hbm, matrix_hbm, columns_hbm, out_ref, own_ref, sources_ref, matrix_ref, columns_ref, sems):
    rows, cols = matrix_ref.shape
    width = sources_ref.shape[1]
    parts, each, wide = out_ref.shape
    myself = grid_row()
    quarter = rows // 4
    small = [
        pltpu.make_async_copy(sources_hbm, sources_ref, sems.at[0]),
        pltpu.make_async_copy(columns_hbm, columns_ref, sems.at[1]),
    ]
    large = []
    for at in range(4):
        here = pl.ds(at * quarter, quarter)
        large.append(pltpu.make_async_copy(matrix_hbm.at[here], matrix_ref.at[here], sems.at[2 + at]))
    for copy in small + large:
        copy.start()
    for copy in small:
        copy.wait()

    columns = columns_ref[...]
    own_ref[...] = columns.astype(HALF)
    columns = columns * SCALE
    picks = one_hot(as_column(sources_ref[...]) - myself * rows == iota((width, rows), 1))
    for copy in large:
        copy.wait()
    block = matrix_ref[...]
    power = range_power(block)
    block = (block * jnp.exp2(power)).astype(HALF)
    corner = (iota((each, wide - cols), 0) == 0) & (iota((each, wide - cols), 1) == 0)
    holders = columns.shape[0] // 4
    for holder in range(holders):
        high = 4 * holder
        piece = jnp.concatenate([columns[high : high + 4, 128 * q : 128 * q + 128] for q in range(4)], axis=0)
        piece = jnp.where(corner, power, piece)
        for part in range(holder, parts, holders):
            out_ref[part, :, cols:wide] = piece

    @pl.when(myself == 0)
    def _():
        out_ref[:, :, 0:cols] = block.astype(jnp.float32).reshape(parts, each, cols)

    @pl.when(myself != 0)
    def _():
        out_ref[:, :, 0:cols] = half_dot(picks, block).reshape(parts, each, cols)


def collect_kernel(got_ref, out_ref):
    parts, each, twice = out_ref.shape
    cols = twice // 2
    factors = jnp.exp2(-got_ref[:, 0:1, cols : cols + 1])
    total = got_ref[1, :, 0:cols] * factors[1]
    for part in range(2, parts):
        total = total + got_ref[part, :, 0:cols] * factors[part]
    pivots = total.astype(HALF)
    top = (got_ref[0, :, 0:cols] * factors[0]).astype(HALF)
    for part in range(parts):
        out_ref[part, :, 0:cols] = pivots
        out_ref[part, :, cols:twice] = top


def invert_block(lower):
    n = lower.shape[0]
    row, col = iota((n, n), 0), iota((n, n), 1)
    unit = jnp.where(row == col, 1.0, 0.0)
    power = jnp.where((row // 32 == col // 32) & (row > col), lower, 0.0)
    inverse = unit - power
    for _ in range(4):
        power = exact_dot(power, power)
        inverse = inverse + exact_dot(inverse, power)
    size = 32
    while size < n:
        off = (row // (2 * size) == col // (2 * size)) & (row // size > col // size)
        below = jnp.where(off, lower, 0.0)
        inverse = inverse - exact_dot(inverse, exact_dot(below, inverse))
        size *= 2
    return inverse


def invert_kernel(mine_ref, other_ref, below_ref, inverse_ref, lower_ref):
    width = lower_ref.shape[0]
    core = lax.axis_index("core")
    mine, other = mine_ref[...], other_ref[...]
    pair = (jnp.where(core == 0, mine, other), jnp.where(core == 0, other, mine))
    lines = []
    for at in range(8):
        for half in pair:
            lanes = []
            for q in range(4):
                lanes.append(jnp.concatenate([half[8 * x + at, 4 * q : 4 * q + 4] for x in range(8)], axis=0))
            lines.append(jnp.concatenate(lanes, axis=1))
    lower_ref[...] = jnp.transpose(jnp.concatenate(lines, axis=0)) * (1.0 / SCALE)

    count = width // 128
    inverses = []
    for block in range(count):
        here = slice(128 * block, 128 * block + 128)
        inverses.append(invert_block(lower_ref[here, here]))
        inverse_ref[:, block] = in_two(inverses[block])
    for at, block, place in STEPS:
        here = slice(128 * block, 128 * block + 128)
        below_ref[:, place] = in_two(-exact_dot(inverses[block], lower_ref[here, 128 * at : 128 * at + 128]))


def weights_kernel(own_ref, across_ref, weights_ref, gathered_ref):
    core, chip = lax.axis_index("core"), lax.axis_index("y")
    for at, ahead in enumerate(ARRIVALS):
        start = 64 * lax.rem(chip + ahead, 8)
        here = slice(32 * at, 32 * at + 32)
        gathered_ref[pl.ds(pl.multiple_of(start + 32 * core, 32), 32), :] = own_ref[here, :]
        gathered_ref[pl.ds(pl.multiple_of(start + 32 * (1 - core), 32), 32), :] = across_ref[here, :]
    weights_ref[...] = -jnp.transpose(gathered_ref[...])


def choose_kernel(sources_ref, matrix_ref, choose_ref, kept_ref):
    width = sources_ref.shape[1]
    sources = sources_ref[...]
    rows, cols = matrix_ref.shape
    lands = one_hot(sources - grid_row() * rows == iota((rows, width), 0))
    landed = half_dot(lands, jnp.ones((width, 128), HALF))
    kept_ref[...] = jnp.where(jnp.concatenate([landed] * (cols // 128), axis=1) > 0.5, 0.0, matrix_ref[...])

    sources_column = as_column(sources)
    square = (width, width)
    chosen = one_hot(sources_column == iota(square, 1))
    used = half_dot(jnp.ones((8, width), HALF), chosen)
    before = one_hot(iota(square, 0) <= iota(square, 1))
    free = 1.0 - used
    free_rank = half_dot(free.astype(HALF), before)
    vacated = jnp.broadcast_to(jnp.where(sources >= width, 1.0, 0.0), (8, width))
    vacated_rank = half_dot(vacated.astype(HALF), before)
    rank_column = jnp.transpose(vacated_rank)[:, 0:1]
    match = (free_rank[0:1] == rank_column) & (free[0:1] > 0.5) & (sources_column >= width)
    choose_ref[...] = chosen + one_hot(match)


def finish_kernel(
    sources_ref, got_ref, kept_ref, below_ref, inverse_ref, weights_ref, choose_ref, out_hbm, out_ref, sems
):
    rows, cols = kept_ref.shape
    width = sources_ref.shape[1]
    myself = grid_row()
    sources = sources_ref[...]
    moved = half_dot(choose_ref[...], got_ref[:, :, cols : 2 * cols].reshape(width, cols))
    found = got_ref[:, :, 0:cols].reshape(width, cols).astype(jnp.float32)
    pivots = jnp.where(as_column(sources) >= width, found, moved)
    count = width // 128
    upper = []
    for block in range(count):
        upper.append(split_dot(inverse_ref[:, block], pivots[128 * block : 128 * block + 128]))
    first = 0
    for at in range(count - 1):
        more = count - 1 - at
        change = split_dot(below_ref[:, first : first + more].reshape(2, 128 * more, 128), upper[at])
        for block in range(more):
            upper[at + 1 + block] = upper[at + 1 + block] + change[128 * block : 128 * block + 128]
        first += more
    upper = jnp.concatenate(upper, axis=0)

    quarter = rows // 4
    copies = []
    for at in range(4):
        here = pl.ds(at * quarter, quarter)
        copies.append(pltpu.make_async_copy(out_ref.at[here], out_hbm.at[here], sems.at[at]))

    @pl.when(myself == 0)
    def _():
        for at in range(4):
            here = slice(at * quarter, at * quarter + quarter)
            out_ref[here, :] = upper[here]
            copies[at].start()

    @pl.when(myself != 0)
    def _():
        fills, half = moved.astype(HALF), upper.astype(HALF)
        for at in range(4):
            here = slice(at * quarter, at * quarter + quarter)
            lands = one_hot(sources - (myself * rows + at * quarter) == iota((quarter, width), 0))
            change = half_dot(lands, fills) + half_dot(weights_ref[here, :], half)
            out_ref[here, :] = kept_ref[here, :] + change
            copies[at].start()

    for copy in copies:
        copy.wait()


def everyone(block, count):
    return jnp.broadcast_to(block[None], (count,) + block.shape)


def exchange(blocks, axes):
    return lax.all_to_all(blocks, axes, 0, 0, tiled=False)


def on_device(matrix, panel, sources):
    rows, cols = matrix.shape
    width = sources.shape[0]
    parts = lax.axis_size(GRID_ROW)
    chips = lax.axis_size("y")
    each = width // parts
    f32 = jnp.float32
    sources = sources.reshape(1, width)
    columns = panel.T
    vmem = pl.BlockSpec(memory_space=pltpu.VMEM)
    hbm = pl.BlockSpec(memory_space=pltpu.HBM)

    offer, own = call(
        offer_kernel,
        (jax.ShapeDtypeStruct((parts, each, cols + 128), f32), jax.ShapeDtypeStruct(columns.shape, HALF)),
        2 * width * rows * cols,
        2 * rows * cols * 4,
        in_specs=[hbm, hbm, hbm],
        scratch_shapes=[
            pltpu.VMEM((1, width), jnp.int32),
            pltpu.VMEM((rows, cols), f32),
            pltpu.VMEM(columns.shape, f32),
            pltpu.SemaphoreType.DMA((6,)),
        ],
    )(in_hbm(sources), in_hbm(matrix), in_hbm(columns))
    got = exchange(offer.astype(SHORT), GRID_ROW)

    choose, kept = call(
        choose_kernel,
        (jax.ShapeDtypeStruct((width, width), HALF), jax.ShapeDtypeStruct((rows, cols), f32)),
        4 * width * width * width,
        4 * rows * cols * 4,
    )(sources, matrix)

    def bring(block, ahead):
        return lax.ppermute(block, "y", [(i, (i - ahead) % chips) for i in range(chips)])

    came = [bring(own, 4), bring(own, 2)]
    piece = got[0, :, cols:]
    piece, came, choose, kept = lax.optimization_barrier((piece, came, choose, kept))
    mine = exchange(everyone(piece, 8 * chips), ("x", "y"))

    collected = call(
        collect_kernel, jax.ShapeDtypeStruct((parts, each, 2 * cols), HALF), parts * each * cols, 4 * parts * each * cols
    )(got.astype(f32))
    three = jnp.concatenate([own] + came, axis=0)
    came = bring(three, 1)
    collected, mine, came = lax.optimization_barrier((collected, mine, came))
    last = bring(jnp.concatenate([own, came[0:32]], axis=0), 6)
    arrived = exchange(collected, GRID_ROW)
    other = lax.ppermute(mine, "core", [(0, 1), (1, 0)])

    below, inverse = call(
        invert_kernel,
        (jax.ShapeDtypeStruct((2, 6, 128, 128), HALF), jax.ShapeDtypeStruct((2, 4, 128, 128), HALF)),
        10 * width * width * width,
        8 * width * width * 4,
        scratch_shapes=[pltpu.VMEM((width, width), f32)],
    )(mine.astype(f32), other.astype(f32))
    last, inverse = lax.optimization_barrier((last, inverse))
    own = jnp.concatenate([three, came, last], axis=0)
    across = lax.ppermute(own, "core", [(0, 1), (1, 0)])
    weights = call(
        weights_kernel,
        jax.ShapeDtypeStruct((rows, width), HALF),
        width * rows,
        4 * width * rows,
        scratch_shapes=[pltpu.VMEM((width, rows), HALF)],
    )(own, across)
    return call(
        finish_kernel,
        jax.ShapeDtypeStruct((rows, cols), f32),
        8 * rows * cols * width,
        12 * rows * cols * 4,
        in_specs=[vmem] * 7,
        out_specs=hbm,
        scratch_shapes=[pltpu.VMEM((rows, cols), f32), pltpu.SemaphoreType.DMA((4,))],
    )(sources, arrived, kept, below, inverse, weights, choose)


def solution(mesh):
    shape = mesh.devices.shape
    chips = mesh.devices.reshape(shape[0] // 8, 8, shape[1] // 2, 2)
    grid = Mesh(chips, ("z", "x", "y", "core"))
    spec = P(GRID_ROW, ("y", "core"))
    return jax.shard_map(on_device, mesh=grid, in_specs=(spec, spec, P()), out_specs=spec, check_vma=False)
```

```python
import jax
import jax.numpy as jnp
from jax import lax
from jax.experimental import pallas as pl
from jax.experimental.pallas import tpu as pltpu
from jax.sharding import Mesh, PartitionSpec as P

GRID_ROW = ("z", "x")
SCALE = 65536.0
ARRIVALS = (0, 4, 2, 1, 5, 3, 6, 7)
STEPS = ((0, 1, 0), (0, 2, 1), (0, 3, 2), (1, 2, 3), (1, 3, 4), (2, 3, 5))
VMEM_LIMIT = 20 * 1024 * 1024
HALF = jnp.bfloat16
SHORT = jnp.float16


def call(kernel, out_shape, flops, moved, **more):
    return pl.pallas_call(
        kernel,
        out_shape=out_shape,
        **more,
        compiler_params=pltpu.CompilerParams(vmem_limit_bytes=VMEM_LIMIT),
        cost_estimate=pl.CostEstimate(flops=flops, bytes_accessed=moved, transcendentals=0),
    )


def in_hbm(array):
    return pltpu.with_memory_space_constraint(array, pltpu.HBM)


def grid_row():
    return lax.axis_index("z") * lax.axis_size("x") + lax.axis_index("x")


def exact_dot(left, right):
    return jnp.dot(left, right, precision=lax.Precision.HIGHEST, preferred_element_type=jnp.float32)


def half_dot(left, right):
    return jnp.dot(left, right, preferred_element_type=jnp.float32)


def in_two(values):
    high = values.astype(HALF)
    low = (values - high.astype(jnp.float32)).astype(HALF)
    return jnp.stack([high, low])


def split_dot(left, right):
    high = right.astype(HALF)
    low = (right - high.astype(jnp.float32)).astype(HALF)
    sides = jnp.concatenate([left[0], left[1], left[0]], axis=1)
    return half_dot(sides, jnp.concatenate([high, high, low], axis=0))


def iota(shape, dim):
    return lax.broadcasted_iota(jnp.int32, shape, dim)


def as_column(row):
    return jnp.transpose(jnp.broadcast_to(row, (8, row.shape[1])))[:, 0:1]


def one_hot(hit):
    return jnp.where(hit, 1.0, 0.0).astype(HALF)


def range_power(block):
    largest = jnp.maximum(jnp.max(jnp.abs(block)), 1e-30)
    return 13.0 - jnp.ceil(jnp.log2(jnp.full((1, 1), largest, jnp.float32)))


def offer_kernel(sources_hbm, matrix_hbm, columns_hbm, out_ref, own_ref, sources_ref, matrix_ref, columns_ref, sems):
    rows, cols = matrix_ref.shape
    width = sources_ref.shape[1]
    parts, each, wide = out_ref.shape
    myself = grid_row()
    quarter = rows // 4
    small = [
        pltpu.make_async_copy(sources_hbm, sources_ref, sems.at[0]),
        pltpu.make_async_copy(columns_hbm, columns_ref, sems.at[1]),
    ]
    large = []
    for at in range(4):
        here = pl.ds(at * quarter, quarter)
        large.append(pltpu.make_async_copy(matrix_hbm.at[here], matrix_ref.at[here], sems.at[2 + at]))
    for copy in small + large:
        copy.start()
    for copy in small:
        copy.wait()

    columns = columns_ref[...]
    own_ref[...] = columns.astype(HALF)
    columns = columns * SCALE
    picks = one_hot(as_column(sources_ref[...]) - myself * rows == iota((width, rows), 1))
    for copy in large:
        copy.wait()
    block = matrix_ref[...]
    power = range_power(block)
    block = (block * jnp.exp2(power)).astype(HALF)
    corner = (iota((each, wide - cols), 0) == 0) & (iota((each, wide - cols), 1) == 0)
    holders = columns.shape[0] // 4
    for holder in range(holders):
        high = 4 * holder
        piece = jnp.concatenate([columns[high : high + 4, 128 * q : 128 * q + 128] for q in range(4)], axis=0)
        piece = jnp.where(corner, power, piece)
        for part in range(holder, parts, holders):
            out_ref[part, :, cols:wide] = piece

    @pl.when(myself == 0)
    def _():
        out_ref[:, :, 0:cols] = block.astype(jnp.float32).reshape(parts, each, cols)

    @pl.when(myself != 0)
    def _():
        out_ref[:, :, 0:cols] = half_dot(picks, block).reshape(parts, each, cols)


def collect_kernel(got_ref, out_ref):
    parts, each, twice = out_ref.shape
    cols = twice // 2
    factors = jnp.exp2(-got_ref[:, 0:1, cols : cols + 1])
    total = got_ref[1, :, 0:cols] * factors[1]
    for part in range(2, parts):
        total = total + got_ref[part, :, 0:cols] * factors[part]
    pivots = total.astype(HALF)
    top = (got_ref[0, :, 0:cols] * factors[0]).astype(HALF)
    for part in range(parts):
        out_ref[part, :, 0:cols] = pivots
        out_ref[part, :, cols:twice] = top


def invert_blocks(lowers):
    n = lowers[0].shape[0]
    row, col = iota((n, n), 0), iota((n, n), 1)
    unit = jnp.where(row == col, 1.0, 0.0)
    near = (row // 32 == col // 32) & (row > col)
    powers = [jnp.where(near, lower, 0.0) for lower in lowers]
    inverses = [unit - power for power in powers]
    for _ in range(4):
        powers = [exact_dot(power, power) for power in powers]
        inverses = [inverse + exact_dot(inverse, power) for inverse, power in zip(inverses, powers)]
    size = 32
    while size < n:
        off = (row // (2 * size) == col // (2 * size)) & (row // size > col // size)
        turned = [exact_dot(jnp.where(off, lower, 0.0), inverse) for lower, inverse in zip(lowers, inverses)]
        inverses = [inverse - exact_dot(inverse, turn) for inverse, turn in zip(inverses, turned)]
        size *= 2
    return inverses


def invert_kernel(mine_ref, other_ref, below_ref, inverse_ref, lower_ref):
    width = lower_ref.shape[0]
    core = lax.axis_index("core")
    mine, other = mine_ref[...], other_ref[...]
    pair = (jnp.where(core == 0, mine, other), jnp.where(core == 0, other, mine))
    lines = []
    for at in range(8):
        for half in pair:
            lanes = []
            for q in range(4):
                lanes.append(jnp.concatenate([half[8 * x + at, 4 * q : 4 * q + 4] for x in range(8)], axis=0))
            lines.append(jnp.concatenate(lanes, axis=1))
    lower_ref[...] = jnp.transpose(jnp.concatenate(lines, axis=0)) * (1.0 / SCALE)

    count = width // 128

    def block_of(down, across):
        return lower_ref[128 * down : 128 * down + 128, 128 * across : 128 * across + 128]

    inverses = invert_blocks([block_of(at, at) for at in range(count)])
    for at in range(count):
        inverse_ref[:, at] = in_two(inverses[at])
    for at, block, place in STEPS:
        below_ref[:, place] = in_two(-split_dot(in_two(inverses[block]), block_of(block, at)))


def weights_kernel(own_ref, across_ref, weights_ref, gathered_ref):
    core, chip = lax.axis_index("core"), lax.axis_index("y")
    for at, ahead in enumerate(ARRIVALS):
        start = 64 * lax.rem(chip + ahead, 8)
        here = slice(32 * at, 32 * at + 32)
        gathered_ref[pl.ds(pl.multiple_of(start + 32 * core, 32), 32), :] = own_ref[here, :]
        gathered_ref[pl.ds(pl.multiple_of(start + 32 * (1 - core), 32), 32), :] = across_ref[here, :]
    weights_ref[...] = -jnp.transpose(gathered_ref[...])


def choose_kernel(sources_ref, matrix_ref, choose_ref, kept_ref):
    width = sources_ref.shape[1]
    sources = sources_ref[...]
    rows, cols = matrix_ref.shape
    lands = one_hot(sources - grid_row() * rows == iota((rows, width), 0))
    landed = half_dot(lands, jnp.ones((width, 128), HALF))
    kept_ref[...] = jnp.where(jnp.concatenate([landed] * (cols // 128), axis=1) > 0.5, 0.0, matrix_ref[...])

    sources_column = as_column(sources)
    square = (width, width)
    chosen = one_hot(sources_column == iota(square, 1))
    used = half_dot(jnp.ones((8, width), HALF), chosen)
    before = one_hot(iota(square, 0) <= iota(square, 1))
    free = 1.0 - used
    free_rank = half_dot(free.astype(HALF), before)
    vacated = jnp.broadcast_to(jnp.where(sources >= width, 1.0, 0.0), (8, width))
    vacated_rank = half_dot(vacated.astype(HALF), before)
    rank_column = jnp.transpose(vacated_rank)[:, 0:1]
    match = (free_rank[0:1] == rank_column) & (free[0:1] > 0.5) & (sources_column >= width)
    choose_ref[...] = chosen + one_hot(match)


def finish_kernel(
    sources_ref, got_ref, kept_ref, below_ref, inverse_ref, weights_ref, choose_ref, out_hbm, out_ref, sems
):
    rows, cols = kept_ref.shape
    width = sources_ref.shape[1]
    myself = grid_row()
    sources = sources_ref[...]
    moved = half_dot(choose_ref[...], got_ref[:, :, cols : 2 * cols].reshape(width, cols))
    found = got_ref[:, :, 0:cols].reshape(width, cols).astype(jnp.float32)
    pivots = jnp.where(as_column(sources) >= width, found, moved)
    count = width // 128
    upper = []
    for block in range(count):
        upper.append(split_dot(inverse_ref[:, block], pivots[128 * block : 128 * block + 128]))
    first = 0
    for at in range(count - 1):
        more = count - 1 - at
        change = split_dot(below_ref[:, first : first + more].reshape(2, 128 * more, 128), upper[at])
        for block in range(more):
            upper[at + 1 + block] = upper[at + 1 + block] + change[128 * block : 128 * block + 128]
        first += more
    upper = jnp.concatenate(upper, axis=0)

    quarter = rows // 4
    copies = []
    for at in range(4):
        here = pl.ds(at * quarter, quarter)
        copies.append(pltpu.make_async_copy(out_ref.at[here], out_hbm.at[here], sems.at[at]))

    @pl.when(myself == 0)
    def _():
        for at in range(4):
            here = slice(at * quarter, at * quarter + quarter)
            out_ref[here, :] = upper[here]
            copies[at].start()

    @pl.when(myself != 0)
    def _():
        fills, half = moved.astype(HALF), upper.astype(HALF)
        for at in range(4):
            here = slice(at * quarter, at * quarter + quarter)
            lands = one_hot(sources - (myself * rows + at * quarter) == iota((quarter, width), 0))
            change = half_dot(lands, fills) + half_dot(weights_ref[here, :], half)
            out_ref[here, :] = kept_ref[here, :] + change
            copies[at].start()

    for copy in copies:
        copy.wait()


def everyone(block, count):
    return jnp.broadcast_to(block[None], (count,) + block.shape)


def exchange(blocks, axes):
    return lax.all_to_all(blocks, axes, 0, 0, tiled=False)


def on_device(matrix, panel, sources):
    rows, cols = matrix.shape
    width = sources.shape[0]
    parts = lax.axis_size(GRID_ROW)
    chips = lax.axis_size("y")
    each = width // parts
    f32 = jnp.float32
    sources = sources.reshape(1, width)
    columns = panel.T
    vmem = pl.BlockSpec(memory_space=pltpu.VMEM)
    hbm = pl.BlockSpec(memory_space=pltpu.HBM)

    offer, own = call(
        offer_kernel,
        (jax.ShapeDtypeStruct((parts, each, cols + 128), f32), jax.ShapeDtypeStruct(columns.shape, HALF)),
        2 * width * rows * cols,
        2 * rows * cols * 4,
        in_specs=[hbm, hbm, hbm],
        scratch_shapes=[
            pltpu.VMEM((1, width), jnp.int32),
            pltpu.VMEM((rows, cols), f32),
            pltpu.VMEM(columns.shape, f32),
            pltpu.SemaphoreType.DMA((6,)),
        ],
    )(in_hbm(sources), in_hbm(matrix), in_hbm(columns))
    got = exchange(offer.astype(SHORT), GRID_ROW)

    choose, kept = call(
        choose_kernel,
        (jax.ShapeDtypeStruct((width, width), HALF), jax.ShapeDtypeStruct((rows, cols), f32)),
        4 * width * width * width,
        4 * rows * cols * 4,
    )(sources, matrix)

    def bring(block, ahead):
        return lax.ppermute(block, "y", [(i, (i - ahead) % chips) for i in range(chips)])

    came = [bring(own, 4), bring(own, 2)]
    piece = got[0, :, cols:]
    piece, came, choose, kept = lax.optimization_barrier((piece, came, choose, kept))
    mine = exchange(everyone(piece, 8 * chips), ("x", "y"))

    collected = call(
        collect_kernel, jax.ShapeDtypeStruct((parts, each, 2 * cols), HALF), parts * each * cols, 4 * parts * each * cols
    )(got.astype(f32))
    three = jnp.concatenate([own] + came, axis=0)
    came = bring(three, 1)
    collected, mine, came = lax.optimization_barrier((collected, mine, came))
    last = bring(jnp.concatenate([own, came[0:32]], axis=0), 6)
    arrived = exchange(collected, GRID_ROW)
    other = lax.ppermute(mine, "core", [(0, 1), (1, 0)])

    below, inverse = call(
        invert_kernel,
        (jax.ShapeDtypeStruct((2, 6, 128, 128), HALF), jax.ShapeDtypeStruct((2, 4, 128, 128), HALF)),
        10 * width * width * width,
        8 * width * width * 4,
        scratch_shapes=[pltpu.VMEM((width, width), f32)],
    )(mine.astype(f32), other.astype(f32))
    last, inverse = lax.optimization_barrier((last, inverse))
    own = jnp.concatenate([three, came, last], axis=0)
    across = lax.ppermute(own, "core", [(0, 1), (1, 0)])
    weights = call(
        weights_kernel,
        jax.ShapeDtypeStruct((rows, width), HALF),
        width * rows,
        4 * width * rows,
        scratch_shapes=[pltpu.VMEM((width, rows), HALF)],
    )(own, across)
    return call(
        finish_kernel,
        jax.ShapeDtypeStruct((rows, cols), f32),
        8 * rows * cols * width,
        12 * rows * cols * 4,
        in_specs=[vmem] * 7,
        out_specs=hbm,
        scratch_shapes=[pltpu.VMEM((rows, cols), f32), pltpu.SemaphoreType.DMA((4,))],
    )(sources, arrived, kept, below, inverse, weights, choose)


def solution(mesh):
    shape = mesh.devices.shape
    chips = mesh.devices.reshape(shape[0] // 8, 8, shape[1] // 2, 2)
    grid = Mesh(chips, ("z", "x", "y", "core"))
    spec = P(GRID_ROW, ("y", "core"))
    return jax.shard_map(on_device, mesh=grid, in_specs=(spec, spec, P()), out_specs=spec, check_vma=False)
```

```python
import jax
import jax.numpy as jnp
from jax import lax
from jax.experimental import pallas as pl
from jax.experimental.pallas import tpu as pltpu
from jax.sharding import Mesh, PartitionSpec as P

GRID_ROW = ("z", "x")
PARTNERS = ("x", "z")
SCALE = 65536.0
ARRIVALS = (0, 4, 2, 1, 5, 3, 6, 7)
STEPS = ((0, 1, 0), (0, 2, 1), (0, 3, 2), (1, 2, 3), (1, 3, 4), (2, 3, 5))
VMEM_LIMIT = 20 * 1024 * 1024
HALF = jnp.bfloat16
SHORT = jnp.float16


def call(kernel, out_shape, flops, moved, **more):
    return pl.pallas_call(
        kernel,
        out_shape=out_shape,
        **more,
        compiler_params=pltpu.CompilerParams(vmem_limit_bytes=VMEM_LIMIT),
        cost_estimate=pl.CostEstimate(flops=flops, bytes_accessed=moved, transcendentals=0),
    )


def in_hbm(array):
    return pltpu.with_memory_space_constraint(array, pltpu.HBM)


def grid_row():
    return lax.axis_index("z") * lax.axis_size("x") + lax.axis_index("x")


def exact_dot(left, right):
    return jnp.dot(left, right, precision=lax.Precision.HIGHEST, preferred_element_type=jnp.float32)


def half_dot(left, right):
    return jnp.dot(left, right, preferred_element_type=jnp.float32)


def in_two(values):
    high = values.astype(HALF)
    low = (values - high.astype(jnp.float32)).astype(HALF)
    return jnp.stack([high, low])


def split_dot(left, right):
    high = right.astype(HALF)
    low = (right - high.astype(jnp.float32)).astype(HALF)
    sides = jnp.concatenate([left[0], left[1], left[0]], axis=1)
    return half_dot(sides, jnp.concatenate([high, high, low], axis=0))


def iota(shape, dim):
    return lax.broadcasted_iota(jnp.int32, shape, dim)


def as_column(row):
    return jnp.transpose(jnp.broadcast_to(row, (8, row.shape[1])))[:, 0:1]


def one_hot(hit):
    return jnp.where(hit, 1.0, 0.0).astype(HALF)


def range_power(block):
    largest = jnp.maximum(jnp.max(jnp.abs(block)), 1e-30)
    return 13.0 - jnp.ceil(jnp.log2(jnp.full((1, 1), largest, jnp.float32)))


def offer_kernel(sources_hbm, matrix_hbm, columns_hbm, out_ref, own_ref, sources_ref, matrix_ref, columns_ref, sems):
    rows, cols = matrix_ref.shape
    width = sources_ref.shape[1]
    parts, each, wide = out_ref.shape
    myself = grid_row()
    quarter = rows // 4
    small = [
        pltpu.make_async_copy(sources_hbm, sources_ref, sems.at[0]),
        pltpu.make_async_copy(columns_hbm, columns_ref, sems.at[1]),
    ]
    large = []
    for at in range(4):
        here = pl.ds(at * quarter, quarter)
        large.append(pltpu.make_async_copy(matrix_hbm.at[here], matrix_ref.at[here], sems.at[2 + at]))
    for copy in small + large:
        copy.start()
    for copy in small:
        copy.wait()

    columns = columns_ref[...]
    own_ref[...] = columns.astype(HALF)
    columns = columns * SCALE
    picks = one_hot(as_column(sources_ref[...]) - myself * rows == iota((width, rows), 1))
    for copy in large:
        copy.wait()
    block = matrix_ref[...]
    power = range_power(block)
    block = (block * jnp.exp2(power)).astype(HALF)
    corner = (iota((each, wide - cols), 0) == 0) & (iota((each, wide - cols), 1) == 0)
    holders = columns.shape[0] // 4
    planes = parts // holders
    for holder in range(holders):
        high = 4 * holder
        piece = jnp.concatenate([columns[high : high + 4, 128 * q : 128 * q + 128] for q in range(4)], axis=0)
        piece = jnp.where(corner, power, piece)
        for part in range(planes * holder, planes * holder + planes):
            out_ref[part, :, cols:wide] = piece

    @pl.when(myself == 0)
    def _():
        out_ref[:, :, 0:cols] = block.astype(jnp.float32).reshape(parts, each, cols)

    @pl.when(myself != 0)
    def _():
        out_ref[:, :, 0:cols] = half_dot(picks, block).reshape(parts, each, cols)


def collect_kernel(got_ref, out_ref):
    parts, each, twice = out_ref.shape
    cols = twice // 2
    factors = jnp.exp2(-got_ref[:, 0:1, cols : cols + 1])
    total = got_ref[1, :, 0:cols] * factors[1]
    for part in range(2, parts):
        total = total + got_ref[part, :, 0:cols] * factors[part]
    pivots = total.astype(HALF)
    top = (got_ref[0, :, 0:cols] * factors[0]).astype(HALF)
    for part in range(parts):
        out_ref[part, :, 0:cols] = pivots
        out_ref[part, :, cols:twice] = top


def invert_blocks(lowers):
    n = lowers[0].shape[0]
    row, col = iota((n, n), 0), iota((n, n), 1)
    unit = jnp.where(row == col, 1.0, 0.0)
    near = (row // 32 == col // 32) & (row > col)
    powers = [jnp.where(near, lower, 0.0) for lower in lowers]
    inverses = [unit - power for power in powers]
    for _ in range(4):
        powers = [exact_dot(power, power) for power in powers]
        inverses = [inverse + exact_dot(inverse, power) for inverse, power in zip(inverses, powers)]
    size = 32
    while size < n:
        off = (row // (2 * size) == col // (2 * size)) & (row // size > col // size)
        turned = [exact_dot(jnp.where(off, lower, 0.0), inverse) for lower, inverse in zip(lowers, inverses)]
        inverses = [inverse - exact_dot(inverse, turn) for inverse, turn in zip(inverses, turned)]
        size *= 2
    return inverses


def invert_kernel(mine_ref, other_ref, below_ref, inverse_ref, lower_ref):
    width = lower_ref.shape[0]
    core = lax.axis_index("core")
    mine, other = mine_ref[...], other_ref[...]
    pair = (jnp.where(core == 0, mine, other), jnp.where(core == 0, other, mine))
    lines = []
    for at in range(8):
        for half in pair:
            lanes = []
            for q in range(4):
                lanes.append(jnp.concatenate([half[8 * x + at, 4 * q : 4 * q + 4] for x in range(8)], axis=0))
            lines.append(jnp.concatenate(lanes, axis=1))
    lower_ref[...] = jnp.transpose(jnp.concatenate(lines, axis=0)) * (1.0 / SCALE)

    count = width // 128

    def block_of(down, across):
        return lower_ref[128 * down : 128 * down + 128, 128 * across : 128 * across + 128]

    inverses = invert_blocks([block_of(at, at) for at in range(count)])
    for at in range(count):
        inverse_ref[:, at] = in_two(inverses[at])
    for at, block, place in STEPS:
        below_ref[:, place] = in_two(-split_dot(in_two(inverses[block]), block_of(block, at)))


def weights_kernel(own_ref, across_ref, weights_ref, gathered_ref):
    core, chip = lax.axis_index("core"), lax.axis_index("y")
    for at, ahead in enumerate(ARRIVALS):
        start = 64 * lax.rem(chip + ahead, 8)
        here = slice(32 * at, 32 * at + 32)
        gathered_ref[pl.ds(pl.multiple_of(start + 32 * core, 32), 32), :] = own_ref[here, :]
        gathered_ref[pl.ds(pl.multiple_of(start + 32 * (1 - core), 32), 32), :] = across_ref[here, :]
    weights_ref[...] = -jnp.transpose(gathered_ref[...])


def choose_kernel(sources_ref, matrix_ref, choose_ref, kept_ref):
    width = sources_ref.shape[1]
    sources = sources_ref[...]
    rows, cols = matrix_ref.shape
    lands = one_hot(sources - grid_row() * rows == iota((rows, width), 0))
    landed = half_dot(lands, jnp.ones((width, 128), HALF))
    kept_ref[...] = jnp.where(jnp.concatenate([landed] * (cols // 128), axis=1) > 0.5, 0.0, matrix_ref[...])

    sources_column = as_column(sources)
    square = (width, width)
    chosen = one_hot(sources_column == iota(square, 1))
    used = half_dot(jnp.ones((8, width), HALF), chosen)
    before = one_hot(iota(square, 0) <= iota(square, 1))
    free = 1.0 - used
    free_rank = half_dot(free.astype(HALF), before)
    vacated = jnp.broadcast_to(jnp.where(sources >= width, 1.0, 0.0), (8, width))
    vacated_rank = half_dot(vacated.astype(HALF), before)
    rank_column = jnp.transpose(vacated_rank)[:, 0:1]
    match = (free_rank[0:1] == rank_column) & (free[0:1] > 0.5) & (sources_column >= width)
    choose_ref[...] = chosen + one_hot(match)


def finish_kernel(
    sources_ref, got_ref, kept_ref, below_ref, inverse_ref, weights_ref, choose_ref, out_hbm, out_ref, sems
):
    rows, cols = kept_ref.shape
    width = sources_ref.shape[1]
    myself = grid_row()
    sources = sources_ref[...]
    moved = half_dot(choose_ref[...], got_ref[:, :, cols : 2 * cols].reshape(width, cols))
    found = got_ref[:, :, 0:cols].reshape(width, cols).astype(jnp.float32)
    pivots = jnp.where(as_column(sources) >= width, found, moved)
    count = width // 128
    upper = []
    for block in range(count):
        upper.append(split_dot(inverse_ref[:, block], pivots[128 * block : 128 * block + 128]))
    first = 0
    for at in range(count - 1):
        more = count - 1 - at
        change = split_dot(below_ref[:, first : first + more].reshape(2, 128 * more, 128), upper[at])
        for block in range(more):
            upper[at + 1 + block] = upper[at + 1 + block] + change[128 * block : 128 * block + 128]
        first += more
    upper = jnp.concatenate(upper, axis=0)

    quarter = rows // 4
    copies = []
    for at in range(4):
        here = pl.ds(at * quarter, quarter)
        copies.append(pltpu.make_async_copy(out_ref.at[here], out_hbm.at[here], sems.at[at]))

    @pl.when(myself == 0)
    def _():
        for at in range(4):
            here = slice(at * quarter, at * quarter + quarter)
            out_ref[here, :] = upper[here]
            copies[at].start()

    @pl.when(myself != 0)
    def _():
        fills, half = moved.astype(HALF), upper.astype(HALF)
        for at in range(4):
            here = slice(at * quarter, at * quarter + quarter)
            lands = one_hot(sources - (myself * rows + at * quarter) == iota((quarter, width), 0))
            change = half_dot(lands, fills) + half_dot(weights_ref[here, :], half)
            out_ref[here, :] = kept_ref[here, :] + change
            copies[at].start()

    for copy in copies:
        copy.wait()


def everyone(block, count):
    return jnp.broadcast_to(block[None], (count,) + block.shape)


def exchange(blocks, axes):
    return lax.all_to_all(blocks, axes, 0, 0, tiled=False)


def on_device(matrix, panel, sources):
    rows, cols = matrix.shape
    width = sources.shape[0]
    parts = lax.axis_size(GRID_ROW)
    chips = lax.axis_size("y")
    each = width // parts
    f32 = jnp.float32
    sources = sources.reshape(1, width)
    columns = panel.T
    vmem = pl.BlockSpec(memory_space=pltpu.VMEM)
    hbm = pl.BlockSpec(memory_space=pltpu.HBM)

    offer, own = call(
        offer_kernel,
        (jax.ShapeDtypeStruct((parts, each, cols + 128), f32), jax.ShapeDtypeStruct(columns.shape, HALF)),
        2 * width * rows * cols,
        2 * rows * cols * 4,
        in_specs=[hbm, hbm, hbm],
        scratch_shapes=[
            pltpu.VMEM((1, width), jnp.int32),
            pltpu.VMEM((rows, cols), f32),
            pltpu.VMEM(columns.shape, f32),
            pltpu.SemaphoreType.DMA((6,)),
        ],
    )(in_hbm(sources), in_hbm(matrix), in_hbm(columns))
    got = exchange(offer.astype(SHORT), PARTNERS)

    choose, kept = call(
        choose_kernel,
        (jax.ShapeDtypeStruct((width, width), HALF), jax.ShapeDtypeStruct((rows, cols), f32)),
        4 * width * width * width,
        4 * rows * cols * 4,
    )(sources, matrix)

    def bring(block, ahead):
        return lax.ppermute(block, "y", [(i, (i - ahead) % chips) for i in range(chips)])

    came = [bring(own, 4), bring(own, 2)]
    piece = got[0, :, cols:]
    piece, came, choose, kept = lax.optimization_barrier((piece, came, choose, kept))
    mine = exchange(everyone(piece, 8 * chips), ("x", "y"))

    collected = call(
        collect_kernel, jax.ShapeDtypeStruct((parts, each, 2 * cols), HALF), parts * each * cols, 4 * parts * each * cols
    )(got.astype(f32))
    three = jnp.concatenate([own] + came, axis=0)
    came = bring(three, 1)
    collected, mine, came = lax.optimization_barrier((collected, mine, came))
    last = bring(jnp.concatenate([own, came[0:32]], axis=0), 6)
    arrived = exchange(collected, PARTNERS)
    other = lax.ppermute(mine, "core", [(0, 1), (1, 0)])

    below, inverse = call(
        invert_kernel,
        (jax.ShapeDtypeStruct((2, 6, 128, 128), HALF), jax.ShapeDtypeStruct((2, 4, 128, 128), HALF)),
        10 * width * width * width,
        8 * width * width * 4,
        scratch_shapes=[pltpu.VMEM((width, width), f32)],
    )(mine.astype(f32), other.astype(f32))
    last, inverse = lax.optimization_barrier((last, inverse))
    own = jnp.concatenate([three, came, last], axis=0)
    across = lax.ppermute(own, "core", [(0, 1), (1, 0)])
    weights = call(
        weights_kernel,
        jax.ShapeDtypeStruct((rows, width), HALF),
        width * rows,
        4 * width * rows,
        scratch_shapes=[pltpu.VMEM((width, rows), HALF)],
    )(own, across)
    return call(
        finish_kernel,
        jax.ShapeDtypeStruct((rows, cols), f32),
        8 * rows * cols * width,
        12 * rows * cols * 4,
        in_specs=[vmem] * 7,
        out_specs=hbm,
        scratch_shapes=[pltpu.VMEM((rows, cols), f32), pltpu.SemaphoreType.DMA((4,))],
    )(sources, arrived, kept, below, inverse, weights, choose)


def solution(mesh):
    shape = mesh.devices.shape
    chips = mesh.devices.reshape(shape[0] // 8, 8, shape[1] // 2, 2)
    grid = Mesh(chips, ("z", "x", "y", "core"))
    spec = P(GRID_ROW, ("y", "core"))
    return jax.shard_map(on_device, mesh=grid, in_specs=(spec, spec, P()), out_specs=spec, check_vma=False)
```

```python
import jax
import jax.numpy as jnp
from jax import lax
from jax.experimental import pallas as pl
from jax.experimental.pallas import tpu as pltpu
from jax.sharding import Mesh, PartitionSpec as P

GRID_ROW = ("z", "x")
PARTNERS = ("x", "z")
SCALE = 65536.0
ARRIVALS = (0, 4, 2, 1, 5, 3, 6, 7)
STEPS = ((0, 1, 0), (0, 2, 1), (0, 3, 2), (1, 2, 3), (1, 3, 4), (2, 3, 5))
VMEM_LIMIT = 20 * 1024 * 1024
HALF = jnp.bfloat16
SHORT = jnp.float16


def call(kernel, out_shape, flops, moved, **more):
    return pl.pallas_call(
        kernel,
        out_shape=out_shape,
        **more,
        compiler_params=pltpu.CompilerParams(vmem_limit_bytes=VMEM_LIMIT),
        cost_estimate=pl.CostEstimate(flops=flops, bytes_accessed=moved, transcendentals=0),
    )


def in_hbm(array):
    return pltpu.with_memory_space_constraint(array, pltpu.HBM)


def grid_row():
    return lax.axis_index("z") * lax.axis_size("x") + lax.axis_index("x")


def exact_dot(left, right):
    return jnp.dot(left, right, precision=lax.Precision.HIGHEST, preferred_element_type=jnp.float32)


def half_dot(left, right):
    return jnp.dot(left, right, preferred_element_type=jnp.float32)


def in_two(values):
    high = values.astype(HALF)
    low = (values - high.astype(jnp.float32)).astype(HALF)
    return jnp.stack([high, low])


def split_dot(left, right):
    high = right.astype(HALF)
    low = (right - high.astype(jnp.float32)).astype(HALF)
    sides = jnp.concatenate([left[0], left[1], left[0]], axis=1)
    return half_dot(sides, jnp.concatenate([high, high, low], axis=0))


def iota(shape, dim):
    return lax.broadcasted_iota(jnp.int32, shape, dim)


def as_column(row):
    return jnp.transpose(jnp.broadcast_to(row, (8, row.shape[1])))[:, 0:1]


def one_hot(hit):
    return jnp.where(hit, 1.0, 0.0).astype(HALF)


def range_power(block):
    largest = jnp.maximum(jnp.max(jnp.abs(block)), 1e-30)
    return 13.0 - jnp.ceil(jnp.log2(jnp.full((1, 1), largest, jnp.float32)))


def offer_kernel(sources_hbm, matrix_hbm, columns_hbm, out_ref, own_ref, sources_ref, matrix_ref, columns_ref, sems):
    rows, cols = matrix_ref.shape
    width = sources_ref.shape[1]
    parts, each, wide = out_ref.shape
    myself = grid_row()
    quarter = rows // 4
    small = [
        pltpu.make_async_copy(sources_hbm, sources_ref, sems.at[0]),
        pltpu.make_async_copy(columns_hbm, columns_ref, sems.at[1]),
    ]
    large = []
    for at in range(4):
        here = pl.ds(at * quarter, quarter)
        large.append(pltpu.make_async_copy(matrix_hbm.at[here], matrix_ref.at[here], sems.at[2 + at]))
    for copy in small + large:
        copy.start()
    for copy in small:
        copy.wait()

    columns = columns_ref[...]
    own_ref[...] = columns.astype(HALF)
    columns = columns * SCALE
    picks = one_hot(as_column(sources_ref[...]) - myself * rows == iota((width, rows), 1))
    for copy in large:
        copy.wait()
    block = matrix_ref[...]
    power = range_power(block)
    block = (block * jnp.exp2(power)).astype(HALF)
    corner = (iota((each, wide - cols), 0) == 0) & (iota((each, wide - cols), 1) == 0)
    holders = columns.shape[0] // 4
    planes = parts // holders
    for holder in range(holders):
        high = 4 * holder
        piece = jnp.concatenate([columns[high : high + 4, 128 * q : 128 * q + 128] for q in range(4)], axis=0)
        piece = jnp.where(corner, power, piece)
        for part in range(planes * holder, planes * holder + planes):
            out_ref[part, :, cols:wide] = piece

    @pl.when(myself == 0)
    def _():
        out_ref[:, :, 0:cols] = block.astype(jnp.float32).reshape(parts, each, cols)

    @pl.when(myself != 0)
    def _():
        out_ref[:, :, 0:cols] = half_dot(picks, block).reshape(parts, each, cols)


def collect_kernel(got_ref, out_ref):
    parts, each, twice = out_ref.shape
    cols = twice // 2
    factors = jnp.exp2(-got_ref[:, 0:1, cols : cols + 1])
    total = got_ref[1, :, 0:cols] * factors[1]
    for part in range(2, parts):
        total = total + got_ref[part, :, 0:cols] * factors[part]
    pivots = total.astype(HALF)
    top = (got_ref[0, :, 0:cols] * factors[0]).astype(HALF)
    for part in range(parts):
        out_ref[part, :, 0:cols] = pivots
        out_ref[part, :, cols:twice] = top


def invert_blocks(lowers):
    n = lowers[0].shape[0]
    row, col = iota((n, n), 0), iota((n, n), 1)
    unit = jnp.where(row == col, 1.0, 0.0)
    near = (row // 32 == col // 32) & (row > col)
    powers = [jnp.where(near, lower, 0.0) for lower in lowers]
    inverses = [unit - power for power in powers]
    for _ in range(4):
        powers = [exact_dot(power, power) for power in powers]
        inverses = [inverse + exact_dot(inverse, power) for inverse, power in zip(inverses, powers)]
    size = 32
    while size < n:
        off = (row // (2 * size) == col // (2 * size)) & (row // size > col // size)
        turned = [exact_dot(jnp.where(off, lower, 0.0), inverse) for lower, inverse in zip(lowers, inverses)]
        inverses = [inverse - exact_dot(inverse, turn) for inverse, turn in zip(inverses, turned)]
        size *= 2
    return inverses


def invert_kernel(mine_ref, other_ref, below_ref, inverse_ref, lower_ref):
    width = lower_ref.shape[0]
    core = lax.axis_index("core")
    mine, other = mine_ref[...], other_ref[...]
    pair = (jnp.where(core == 0, mine, other), jnp.where(core == 0, other, mine))
    lines = []
    for at in range(8):
        for half in pair:
            lanes = []
            for q in range(4):
                lanes.append(jnp.concatenate([half[8 * at + x, 4 * q : 4 * q + 4] for x in range(8)], axis=0))
            lines.append(jnp.concatenate(lanes, axis=1))
    lower_ref[...] = jnp.transpose(jnp.concatenate(lines, axis=0)) * (1.0 / SCALE)

    count = width // 128

    def block_of(down, across):
        return lower_ref[128 * down : 128 * down + 128, 128 * across : 128 * across + 128]

    inverses = invert_blocks([block_of(at, at) for at in range(count)])
    for at in range(count):
        inverse_ref[:, at] = in_two(inverses[at])
    for at, block, place in STEPS:
        below_ref[:, place] = in_two(-split_dot(in_two(inverses[block]), block_of(block, at)))


def weights_kernel(own_ref, across_ref, weights_ref, gathered_ref):
    core, chip = lax.axis_index("core"), lax.axis_index("y")
    for at, ahead in enumerate(ARRIVALS):
        start = 64 * lax.rem(chip + ahead, 8)
        here = slice(32 * at, 32 * at + 32)
        gathered_ref[pl.ds(pl.multiple_of(start + 32 * core, 32), 32), :] = own_ref[here, :]
        gathered_ref[pl.ds(pl.multiple_of(start + 32 * (1 - core), 32), 32), :] = across_ref[here, :]
    weights_ref[...] = -jnp.transpose(gathered_ref[...])


def choose_kernel(sources_ref, matrix_ref, choose_ref, kept_ref):
    width = sources_ref.shape[1]
    sources = sources_ref[...]
    rows, cols = matrix_ref.shape
    lands = one_hot(sources - grid_row() * rows == iota((rows, width), 0))
    landed = half_dot(lands, jnp.ones((width, 128), HALF))
    kept_ref[...] = jnp.where(jnp.concatenate([landed] * (cols // 128), axis=1) > 0.5, 0.0, matrix_ref[...])

    sources_column = as_column(sources)
    square = (width, width)
    chosen = one_hot(sources_column == iota(square, 1))
    used = half_dot(jnp.ones((8, width), HALF), chosen)
    before = one_hot(iota(square, 0) <= iota(square, 1))
    free = 1.0 - used
    free_rank = half_dot(free.astype(HALF), before)
    vacated = jnp.broadcast_to(jnp.where(sources >= width, 1.0, 0.0), (8, width))
    vacated_rank = half_dot(vacated.astype(HALF), before)
    rank_column = jnp.transpose(vacated_rank)[:, 0:1]
    match = (free_rank[0:1] == rank_column) & (free[0:1] > 0.5) & (sources_column >= width)
    choose_ref[...] = chosen + one_hot(match)


def finish_kernel(
    sources_ref, got_ref, kept_ref, below_ref, inverse_ref, weights_ref, choose_ref, out_hbm, out_ref, sems
):
    rows, cols = kept_ref.shape
    width = sources_ref.shape[1]
    myself = grid_row()
    sources = sources_ref[...]
    moved = half_dot(choose_ref[...], got_ref[:, :, cols : 2 * cols].reshape(width, cols)).astype(HALF)
    found = got_ref[:, :, 0:cols].reshape(width, cols)
    pivots = jnp.where(as_column(sources) >= width, found, moved)
    count = width // 128
    upper = []
    for block in range(count):
        right = pivots[128 * block : 128 * block + 128]
        sides = jnp.concatenate([inverse_ref[0, block], inverse_ref[1, block]], axis=1)
        upper.append(half_dot(sides, jnp.concatenate([right, right], axis=0)))
    first = 0
    for at in range(count - 1):
        more = count - 1 - at
        change = split_dot(below_ref[:, first : first + more].reshape(2, 128 * more, 128), upper[at])
        for block in range(more):
            upper[at + 1 + block] = upper[at + 1 + block] + change[128 * block : 128 * block + 128]
        first += more
    upper = jnp.concatenate(upper, axis=0)

    quarter = rows // 4
    copies = []
    for at in range(4):
        here = pl.ds(at * quarter, quarter)
        copies.append(pltpu.make_async_copy(out_ref.at[here], out_hbm.at[here], sems.at[at]))

    @pl.when(myself == 0)
    def _():
        for at in range(4):
            here = slice(at * quarter, at * quarter + quarter)
            out_ref[here, :] = upper[here]
            copies[at].start()

    @pl.when(myself != 0)
    def _():
        half = upper.astype(HALF)
        for at in range(4):
            here = slice(at * quarter, at * quarter + quarter)
            lands = one_hot(sources - (myself * rows + at * quarter) == iota((quarter, width), 0))
            change = half_dot(lands, moved) + half_dot(weights_ref[here, :], half)
            out_ref[here, :] = kept_ref[here, :] + change
            copies[at].start()

    for copy in copies:
        copy.wait()


def everyone(block, count):
    return jnp.broadcast_to(block[None], (count,) + block.shape)


def exchange(blocks, axes):
    return lax.all_to_all(blocks, axes, 0, 0, tiled=False)


def on_device(matrix, panel, sources):
    rows, cols = matrix.shape
    width = sources.shape[0]
    parts = lax.axis_size(GRID_ROW)
    chips = lax.axis_size("y")
    each = width // parts
    f32 = jnp.float32
    sources = sources.reshape(1, width)
    columns = panel.T
    vmem = pl.BlockSpec(memory_space=pltpu.VMEM)
    hbm = pl.BlockSpec(memory_space=pltpu.HBM)

    offer, own = call(
        offer_kernel,
        (jax.ShapeDtypeStruct((parts, each, cols + 128), f32), jax.ShapeDtypeStruct(columns.shape, HALF)),
        2 * width * rows * cols,
        2 * rows * cols * 4,
        in_specs=[hbm, hbm, hbm],
        scratch_shapes=[
            pltpu.VMEM((1, width), jnp.int32),
            pltpu.VMEM((rows, cols), f32),
            pltpu.VMEM(columns.shape, f32),
            pltpu.SemaphoreType.DMA((6,)),
        ],
    )(in_hbm(sources), in_hbm(matrix), in_hbm(columns))
    got = exchange(offer.astype(SHORT), PARTNERS)

    choose, kept = call(
        choose_kernel,
        (jax.ShapeDtypeStruct((width, width), HALF), jax.ShapeDtypeStruct((rows, cols), f32)),
        4 * width * width * width,
        4 * rows * cols * 4,
    )(sources, matrix)

    def bring(block, ahead):
        return lax.ppermute(block, "y", [(i, (i - ahead) % chips) for i in range(chips)])

    came = [bring(own, 4), bring(own, 2)]
    piece = got[0, :, cols:]
    piece, came, choose, kept = lax.optimization_barrier((piece, came, choose, kept))
    mine = exchange(everyone(piece, 8 * chips), ("y", "x"))

    collected = call(
        collect_kernel, jax.ShapeDtypeStruct((parts, each, 2 * cols), HALF), parts * each * cols, 4 * parts * each * cols
    )(got.astype(f32))
    three = jnp.concatenate([own] + came, axis=0)
    came = bring(three, 1)
    collected, mine, came = lax.optimization_barrier((collected, mine, came))
    last = bring(jnp.concatenate([own, came[0:32]], axis=0), 6)
    arrived = exchange(collected, PARTNERS)
    other = lax.ppermute(mine, "core", [(0, 1), (1, 0)])

    below, inverse = call(
        invert_kernel,
        (jax.ShapeDtypeStruct((2, 6, 128, 128), HALF), jax.ShapeDtypeStruct((2, 4, 128, 128), HALF)),
        10 * width * width * width,
        8 * width * width * 4,
        scratch_shapes=[pltpu.VMEM((width, width), f32)],
    )(mine.astype(f32), other.astype(f32))
    last, inverse = lax.optimization_barrier((last, inverse))
    own = jnp.concatenate([three, came, last], axis=0)
    across = lax.ppermute(own, "core", [(0, 1), (1, 0)])
    weights = call(
        weights_kernel,
        jax.ShapeDtypeStruct((rows, width), HALF),
        width * rows,
        4 * width * rows,
        scratch_shapes=[pltpu.VMEM((width, rows), HALF)],
    )(own, across)
    return call(
        finish_kernel,
        jax.ShapeDtypeStruct((rows, cols), f32),
        8 * rows * cols * width,
        12 * rows * cols * 4,
        in_specs=[vmem] * 7,
        out_specs=hbm,
        scratch_shapes=[pltpu.VMEM((rows, cols), f32), pltpu.SemaphoreType.DMA((4,))],
    )(sources, arrived, kept, below, inverse, weights, choose)


def solution(mesh):
    shape = mesh.devices.shape
    chips = mesh.devices.reshape(shape[0] // 8, 8, shape[1] // 2, 2)
    grid = Mesh(chips, ("z", "x", "y", "core"))
    spec = P(GRID_ROW, ("y", "core"))
    return jax.shard_map(on_device, mesh=grid, in_specs=(spec, spec, P()), out_specs=spec, check_vma=False)
```

```python
import jax
import jax.numpy as jnp
from jax import lax
from jax.experimental import pallas as pl
from jax.experimental.pallas import tpu as pltpu
from jax.sharding import Mesh, PartitionSpec as P

GRID_ROW = ("z", "x")
PARTNERS = ("x", "z")
SCALE = 65536.0
ARRIVALS = (0, 4, 2, 1, 5, 3, 6, 7)
STEPS = ((0, 1, 0), (0, 2, 1), (0, 3, 2), (1, 2, 3), (1, 3, 4), (2, 3, 5))
VMEM_LIMIT = 20 * 1024 * 1024
HALF = jnp.bfloat16
SHORT = jnp.float16


def call(kernel, out_shape, flops, moved, **more):
    return pl.pallas_call(
        kernel,
        out_shape=out_shape,
        **more,
        compiler_params=pltpu.CompilerParams(vmem_limit_bytes=VMEM_LIMIT),
        cost_estimate=pl.CostEstimate(flops=flops, bytes_accessed=moved, transcendentals=0),
    )


def in_hbm(array):
    return pltpu.with_memory_space_constraint(array, pltpu.HBM)


def grid_row():
    return lax.axis_index("z") * lax.axis_size("x") + lax.axis_index("x")


def exact_dot(left, right):
    return jnp.dot(left, right, precision=lax.Precision.HIGHEST, preferred_element_type=jnp.float32)


def half_dot(left, right):
    return jnp.dot(left, right, preferred_element_type=jnp.float32)


def in_two(values):
    high = values.astype(HALF)
    low = (values - high.astype(jnp.float32)).astype(HALF)
    return jnp.stack([high, low])


def split_dot(left, right):
    high = right.astype(HALF)
    low = (right - high.astype(jnp.float32)).astype(HALF)
    sides = jnp.concatenate([left[0], left[1], left[0]], axis=1)
    return half_dot(sides, jnp.concatenate([high, high, low], axis=0))


def iota(shape, dim):
    return lax.broadcasted_iota(jnp.int32, shape, dim)


def as_column(row):
    return jnp.transpose(jnp.broadcast_to(row, (8, row.shape[1])))[:, 0:1]


def one_hot(hit):
    return jnp.where(hit, 1.0, 0.0).astype(HALF)


def range_power(block):
    largest = jnp.maximum(jnp.max(jnp.abs(block)), 1e-30)
    return 13.0 - jnp.ceil(jnp.log2(jnp.full((1, 1), largest, jnp.float32)))


def offer_kernel(sources_hbm, matrix_hbm, columns_hbm, out_ref, own_ref, sources_ref, matrix_ref, columns_ref, sems):
    rows, cols = matrix_ref.shape
    width = sources_ref.shape[1]
    parts, each, wide = out_ref.shape
    myself = grid_row()
    quarter = rows // 4
    small = [
        pltpu.make_async_copy(sources_hbm, sources_ref, sems.at[0]),
        pltpu.make_async_copy(columns_hbm, columns_ref, sems.at[1]),
    ]
    large = []
    for at in range(4):
        here = pl.ds(at * quarter, quarter)
        large.append(pltpu.make_async_copy(matrix_hbm.at[here], matrix_ref.at[here], sems.at[2 + at]))
    for copy in small + large:
        copy.start()
    for copy in small:
        copy.wait()

    columns = columns_ref[...]
    own_ref[...] = columns.astype(HALF)
    columns = columns * SCALE
    picks = one_hot(as_column(sources_ref[...]) - myself * rows == iota((width, rows), 1))
    holders = columns.shape[0] // 4
    planes = parts // holders
    for holder in range(holders):
        high = 4 * holder
        piece = jnp.concatenate([columns[high : high + 4, 128 * q : 128 * q + 128] for q in range(4)], axis=0)
        for part in range(planes * holder, planes * holder + planes):
            out_ref[part, :, cols:wide] = piece

    for copy in large:
        copy.wait()
    block = matrix_ref[...]
    power = range_power(block)
    for part in range(parts):
        out_ref[part, 0:1, cols : cols + 1] = power
    block = (block * jnp.exp2(power)).astype(HALF)

    @pl.when(myself == 0)
    def _():
        out_ref[:, :, 0:cols] = block.astype(jnp.float32).reshape(parts, each, cols)

    @pl.when(myself != 0)
    def _():
        out_ref[:, :, 0:cols] = half_dot(picks, block).reshape(parts, each, cols)


def collect_kernel(got_ref, out_ref):
    parts, each, twice = out_ref.shape
    cols = twice // 2
    factors = jnp.exp2(-got_ref[:, 0:1, cols : cols + 1])
    total = got_ref[1, :, 0:cols] * factors[1]
    for part in range(2, parts):
        total = total + got_ref[part, :, 0:cols] * factors[part]
    pivots = total.astype(HALF)
    top = (got_ref[0, :, 0:cols] * factors[0]).astype(HALF)
    for part in range(parts):
        out_ref[part, :, 0:cols] = pivots
        out_ref[part, :, cols:twice] = top


def invert_blocks(lowers):
    n = lowers[0].shape[0]
    row, col = iota((n, n), 0), iota((n, n), 1)
    unit = jnp.where(row == col, 1.0, 0.0)
    near = (row // 32 == col // 32) & (row > col)
    powers = [jnp.where(near, lower, 0.0) for lower in lowers]
    inverses = [unit - power for power in powers]
    for _ in range(4):
        powers = [exact_dot(power, power) for power in powers]
        inverses = [inverse + exact_dot(inverse, power) for inverse, power in zip(inverses, powers)]
    size = 32
    while size < n:
        off = (row // (2 * size) == col // (2 * size)) & (row // size > col // size)
        turned = [exact_dot(jnp.where(off, lower, 0.0), inverse) for lower, inverse in zip(lowers, inverses)]
        inverses = [inverse - exact_dot(inverse, turn) for inverse, turn in zip(inverses, turned)]
        size *= 2
    return inverses


def invert_kernel(mine_ref, other_ref, below_ref, inverse_ref, lower_ref):
    width = lower_ref.shape[0]
    core = lax.axis_index("core")
    mine, other = mine_ref[...], other_ref[...]
    pair = (jnp.where(core == 0, mine, other), jnp.where(core == 0, other, mine))
    lines = []
    for at in range(8):
        for half in pair:
            lanes = []
            for q in range(4):
                lanes.append(jnp.concatenate([half[8 * at + x, 4 * q : 4 * q + 4] for x in range(8)], axis=0))
            lines.append(jnp.concatenate(lanes, axis=1))
    lower_ref[...] = jnp.transpose(jnp.concatenate(lines, axis=0)) * (1.0 / SCALE)

    count = width // 128

    def block_of(down, across):
        return lower_ref[128 * down : 128 * down + 128, 128 * across : 128 * across + 128]

    inverses = invert_blocks([block_of(at, at) for at in range(count)])
    for at in range(count):
        inverse_ref[:, at] = in_two(inverses[at])
    for at, block, place in STEPS:
        below_ref[:, place] = in_two(-split_dot(in_two(inverses[block]), block_of(block, at)))


def weights_kernel(own_ref, across_ref, weights_ref, gathered_ref):
    core, chip = lax.axis_index("core"), lax.axis_index("y")
    for at, ahead in enumerate(ARRIVALS):
        start = 64 * lax.rem(chip + ahead, 8)
        here = slice(32 * at, 32 * at + 32)
        gathered_ref[pl.ds(pl.multiple_of(start + 32 * core, 32), 32), :] = own_ref[here, :]
        gathered_ref[pl.ds(pl.multiple_of(start + 32 * (1 - core), 32), 32), :] = across_ref[here, :]
    weights_ref[...] = -jnp.transpose(gathered_ref[...])


def choose_kernel(sources_ref, matrix_ref, choose_ref, kept_ref):
    width = sources_ref.shape[1]
    sources = sources_ref[...]
    rows, cols = matrix_ref.shape
    lands = one_hot(sources - grid_row() * rows == iota((rows, width), 0))
    landed = half_dot(lands, jnp.ones((width, 128), HALF))
    kept_ref[...] = jnp.where(jnp.concatenate([landed] * (cols // 128), axis=1) > 0.5, 0.0, matrix_ref[...])

    sources_column = as_column(sources)
    square = (width, width)
    chosen = one_hot(sources_column == iota(square, 1))
    used = half_dot(jnp.ones((8, width), HALF), chosen)
    before = one_hot(iota(square, 0) <= iota(square, 1))
    free = 1.0 - used
    free_rank = half_dot(free.astype(HALF), before)
    vacated = jnp.broadcast_to(jnp.where(sources >= width, 1.0, 0.0), (8, width))
    vacated_rank = half_dot(vacated.astype(HALF), before)
    rank_column = jnp.transpose(vacated_rank)[:, 0:1]
    match = (free_rank[0:1] == rank_column) & (free[0:1] > 0.5) & (sources_column >= width)
    choose_ref[...] = chosen + one_hot(match)


def finish_kernel(
    sources_ref, got_ref, kept_ref, below_ref, inverse_ref, weights_ref, choose_ref, out_hbm, out_ref, sems
):
    rows, cols = kept_ref.shape
    width = sources_ref.shape[1]
    myself = grid_row()
    sources = sources_ref[...]
    moved = half_dot(choose_ref[...], got_ref[:, :, cols : 2 * cols].reshape(width, cols)).astype(HALF)
    found = got_ref[:, :, 0:cols].reshape(width, cols)
    pivots = jnp.where(as_column(sources) >= width, found, moved)
    count = width // 128
    upper = []
    for block in range(count):
        right = pivots[128 * block : 128 * block + 128]
        sides = jnp.concatenate([inverse_ref[0, block], inverse_ref[1, block]], axis=1)
        upper.append(half_dot(sides, jnp.concatenate([right, right], axis=0)))
    first = 0
    for at in range(count - 1):
        more = count - 1 - at
        change = split_dot(below_ref[:, first : first + more].reshape(2, 128 * more, 128), upper[at])
        for block in range(more):
            upper[at + 1 + block] = upper[at + 1 + block] + change[128 * block : 128 * block + 128]
        first += more
    upper = jnp.concatenate(upper, axis=0)

    quarter = rows // 4
    copies = []
    for at in range(4):
        here = pl.ds(at * quarter, quarter)
        copies.append(pltpu.make_async_copy(out_ref.at[here], out_hbm.at[here], sems.at[at]))

    @pl.when(myself == 0)
    def _():
        for at in range(4):
            here = slice(at * quarter, at * quarter + quarter)
            out_ref[here, :] = upper[here]
            copies[at].start()

    @pl.when(myself != 0)
    def _():
        half = upper.astype(HALF)
        for at in range(4):
            here = slice(at * quarter, at * quarter + quarter)
            lands = one_hot(sources - (myself * rows + at * quarter) == iota((quarter, width), 0))
            change = half_dot(lands, moved) + half_dot(weights_ref[here, :], half)
            out_ref[here, :] = kept_ref[here, :] + change
            copies[at].start()

    for copy in copies:
        copy.wait()


def everyone(block, count):
    return jnp.broadcast_to(block[None], (count,) + block.shape)


def exchange(blocks, axes):
    return lax.all_to_all(blocks, axes, 0, 0, tiled=False)


def on_device(matrix, panel, sources):
    rows, cols = matrix.shape
    width = sources.shape[0]
    parts = lax.axis_size(GRID_ROW)
    chips = lax.axis_size("y")
    each = width // parts
    f32 = jnp.float32
    sources = sources.reshape(1, width)
    columns = panel.T
    vmem = pl.BlockSpec(memory_space=pltpu.VMEM)
    hbm = pl.BlockSpec(memory_space=pltpu.HBM)

    offer, own = call(
        offer_kernel,
        (jax.ShapeDtypeStruct((parts, each, cols + 128), f32), jax.ShapeDtypeStruct(columns.shape, HALF)),
        2 * width * rows * cols,
        2 * rows * cols * 4,
        in_specs=[hbm, hbm, hbm],
        scratch_shapes=[
            pltpu.VMEM((1, width), jnp.int32),
            pltpu.VMEM((rows, cols), f32),
            pltpu.VMEM(columns.shape, f32),
            pltpu.SemaphoreType.DMA((6,)),
        ],
    )(in_hbm(sources), in_hbm(matrix), in_hbm(columns))
    got = exchange(offer.astype(SHORT), PARTNERS)

    choose, kept = call(
        choose_kernel,
        (jax.ShapeDtypeStruct((width, width), HALF), jax.ShapeDtypeStruct((rows, cols), f32)),
        4 * width * width * width,
        4 * rows * cols * 4,
    )(sources, matrix)

    def bring(block, ahead):
        return lax.ppermute(block, "y", [(i, (i - ahead) % chips) for i in range(chips)])

    came = [bring(own, 4), bring(own, 2)]
    piece = got[0, :, cols:]
    piece, came, choose, kept = lax.optimization_barrier((piece, came, choose, kept))
    mine = exchange(everyone(piece, 8 * chips), ("y", "x"))

    collected = call(
        collect_kernel, jax.ShapeDtypeStruct((parts, each, 2 * cols), HALF), parts * each * cols, 4 * parts * each * cols
    )(got.astype(f32))
    three = jnp.concatenate([own] + came, axis=0)
    came = bring(three, 1)
    collected, mine, came = lax.optimization_barrier((collected, mine, came))
    last = bring(jnp.concatenate([own, came[0:32]], axis=0), 6)
    arrived = exchange(collected, PARTNERS)
    other = lax.ppermute(mine, "core", [(0, 1), (1, 0)])

    below, inverse = call(
        invert_kernel,
        (jax.ShapeDtypeStruct((2, 6, 128, 128), HALF), jax.ShapeDtypeStruct((2, 4, 128, 128), HALF)),
        10 * width * width * width,
        8 * width * width * 4,
        scratch_shapes=[pltpu.VMEM((width, width), f32)],
    )(mine.astype(f32), other.astype(f32))
    last, inverse = lax.optimization_barrier((last, inverse))
    own = jnp.concatenate([three, came, last], axis=0)
    across = lax.ppermute(own, "core", [(0, 1), (1, 0)])
    weights = call(
        weights_kernel,
        jax.ShapeDtypeStruct((rows, width), HALF),
        width * rows,
        4 * width * rows,
        scratch_shapes=[pltpu.VMEM((width, rows), HALF)],
    )(own, across)
    return call(
        finish_kernel,
        jax.ShapeDtypeStruct((rows, cols), f32),
        8 * rows * cols * width,
        12 * rows * cols * 4,
        in_specs=[vmem] * 7,
        out_specs=hbm,
        scratch_shapes=[pltpu.VMEM((rows, cols), f32), pltpu.SemaphoreType.DMA((4,))],
    )(sources, arrived, kept, below, inverse, weights, choose)


def solution(mesh):
    shape = mesh.devices.shape
    chips = mesh.devices.reshape(shape[0] // 8, 8, shape[1] // 2, 2)
    grid = Mesh(chips, ("z", "x", "y", "core"))
    spec = P(GRID_ROW, ("y", "core"))
    return jax.shard_map(on_device, mesh=grid, in_specs=(spec, spec, P()), out_specs=spec, check_vma=False)
```

```python
import jax
import jax.numpy as jnp
from jax import lax
from jax.experimental import pallas as pl
from jax.experimental.pallas import tpu as pltpu
from jax.sharding import Mesh, PartitionSpec as P

GRID_ROW = ("z", "x")
PARTNERS = ("x", "z")
SCALE = 65536.0
ARRIVALS = (0, 4, 2, 1, 5, 3, 6, 7)
STEPS = ((0, 1, 0), (0, 2, 1), (0, 3, 2), (1, 2, 3), (1, 3, 4), (2, 3, 5))
VMEM_LIMIT = 20 * 1024 * 1024
HALF = jnp.bfloat16
SHORT = jnp.float16


def call(kernel, out_shape, flops, moved, **more):
    return pl.pallas_call(
        kernel,
        out_shape=out_shape,
        **more,
        compiler_params=pltpu.CompilerParams(vmem_limit_bytes=VMEM_LIMIT),
        cost_estimate=pl.CostEstimate(flops=flops, bytes_accessed=moved, transcendentals=0),
    )


def in_hbm(array):
    return pltpu.with_memory_space_constraint(array, pltpu.HBM)


def grid_row():
    return lax.axis_index("z") * lax.axis_size("x") + lax.axis_index("x")


def exact_dot(left, right):
    return jnp.dot(left, right, precision=lax.Precision.HIGHEST, preferred_element_type=jnp.float32)


def half_dot(left, right):
    return jnp.dot(left, right, preferred_element_type=jnp.float32)


def in_two(values):
    high = values.astype(HALF)
    low = (values - high.astype(jnp.float32)).astype(HALF)
    return jnp.stack([high, low])


def split_dot(left, right):
    high = right.astype(HALF)
    low = (right - high.astype(jnp.float32)).astype(HALF)
    sides = jnp.concatenate([left[0], left[1], left[0]], axis=1)
    return half_dot(sides, jnp.concatenate([high, high, low], axis=0))


def iota(shape, dim):
    return lax.broadcasted_iota(jnp.int32, shape, dim)


def as_column(row):
    return jnp.transpose(jnp.broadcast_to(row, (8, row.shape[1])))[:, 0:1]


def one_hot(hit):
    return jnp.where(hit, 1.0, 0.0).astype(HALF)


def range_power(block):
    largest = jnp.maximum(jnp.max(jnp.abs(block)), 1e-30)
    return 13.0 - jnp.ceil(jnp.log2(jnp.full((1, 1), largest, jnp.float32)))


def offer_kernel(sources_hbm, matrix_hbm, columns_hbm, out_ref, own_ref, sources_ref, matrix_ref, columns_ref, sems):
    rows, cols = matrix_ref.shape
    width = sources_ref.shape[1]
    parts, each, wide = out_ref.shape
    myself = grid_row()
    quarter = rows // 4
    small = [
        pltpu.make_async_copy(sources_hbm, sources_ref, sems.at[0]),
        pltpu.make_async_copy(columns_hbm, columns_ref, sems.at[1]),
    ]
    large = []
    for at in range(4):
        here = pl.ds(at * quarter, quarter)
        large.append(pltpu.make_async_copy(matrix_hbm.at[here], matrix_ref.at[here], sems.at[2 + at]))
    for copy in small[1:] + large + small[:1]:
        copy.start()
    small[1].wait()

    columns = columns_ref[...]
    own_ref[...] = columns.astype(HALF)
    columns = columns * SCALE
    small[0].wait()
    picks = one_hot(as_column(sources_ref[...]) - myself * rows == iota((width, rows), 1))
    holders = columns.shape[0] // 4
    planes = parts // holders
    for holder in range(holders):
        high = 4 * holder
        piece = jnp.concatenate([columns[high : high + 4, 128 * q : 128 * q + 128] for q in range(4)], axis=0)
        for part in range(planes * holder, planes * holder + planes):
            out_ref[part, :, cols:wide] = piece

    for copy in large:
        copy.wait()
    block = matrix_ref[...]
    power = range_power(block)
    for part in range(parts):
        out_ref[part, 0:1, cols : cols + 1] = power
    block = (block * jnp.exp2(power)).astype(HALF)

    @pl.when(myself == 0)
    def _():
        out_ref[:, :, 0:cols] = block.astype(jnp.float32).reshape(parts, each, cols)

    @pl.when(myself != 0)
    def _():
        out_ref[:, :, 0:cols] = half_dot(picks, block).reshape(parts, each, cols)


def collect_kernel(got_ref, out_ref):
    parts, each, twice = out_ref.shape
    cols = twice // 2
    factors = jnp.exp2(-got_ref[:, 0:1, cols : cols + 1])
    total = got_ref[1, :, 0:cols] * factors[1]
    for part in range(2, parts):
        total = total + got_ref[part, :, 0:cols] * factors[part]
    pivots = total.astype(HALF)
    top = (got_ref[0, :, 0:cols] * factors[0]).astype(HALF)
    for part in range(parts):
        out_ref[part, :, 0:cols] = pivots
        out_ref[part, :, cols:twice] = top


def invert_blocks(lowers):
    n = lowers[0].shape[0]
    row, col = iota((n, n), 0), iota((n, n), 1)
    unit = jnp.where(row == col, 1.0, 0.0)
    near = (row // 32 == col // 32) & (row > col)
    powers = [jnp.where(near, lower, 0.0) for lower in lowers]
    inverses = [unit - power for power in powers]
    for _ in range(4):
        powers = [exact_dot(power, power) for power in powers]
        inverses = [inverse + exact_dot(inverse, power) for inverse, power in zip(inverses, powers)]
    size = 32
    while size < n:
        off = (row // (2 * size) == col // (2 * size)) & (row // size > col // size)
        turned = [exact_dot(jnp.where(off, lower, 0.0), inverse) for lower, inverse in zip(lowers, inverses)]
        inverses = [inverse - exact_dot(inverse, turn) for inverse, turn in zip(inverses, turned)]
        size *= 2
    return inverses


def invert_kernel(mine_ref, other_ref, below_ref, inverse_ref, lower_ref):
    width = lower_ref.shape[0]
    core = lax.axis_index("core")
    mine, other = mine_ref[...], other_ref[...]
    pair = (jnp.where(core == 0, mine, other), jnp.where(core == 0, other, mine))
    lines = []
    for at in range(8):
        for half in pair:
            lanes = []
            for q in range(4):
                lanes.append(jnp.concatenate([half[8 * at + x, 4 * q : 4 * q + 4] for x in range(8)], axis=0))
            lines.append(jnp.concatenate(lanes, axis=1))
    lower_ref[...] = jnp.transpose(jnp.concatenate(lines, axis=0)) * (1.0 / SCALE)

    count = width // 128

    def block_of(down, across):
        return lower_ref[128 * down : 128 * down + 128, 128 * across : 128 * across + 128]

    inverses = invert_blocks([block_of(at, at) for at in range(count)])
    for at in range(count):
        inverse_ref[:, at] = in_two(inverses[at])
    for at, block, place in STEPS:
        below_ref[:, place] = in_two(-split_dot(in_two(inverses[block]), block_of(block, at)))


def weights_kernel(own_ref, across_ref, weights_ref, gathered_ref):
    core, chip = lax.axis_index("core"), lax.axis_index("y")
    for at, ahead in enumerate(ARRIVALS):
        start = 64 * lax.rem(chip + ahead, 8)
        here = slice(32 * at, 32 * at + 32)
        gathered_ref[pl.ds(pl.multiple_of(start + 32 * core, 32), 32), :] = own_ref[here, :]
        gathered_ref[pl.ds(pl.multiple_of(start + 32 * (1 - core), 32), 32), :] = across_ref[here, :]
    weights_ref[...] = -jnp.transpose(gathered_ref[...])


def choose_kernel(sources_ref, matrix_ref, choose_ref, kept_ref):
    width = sources_ref.shape[1]
    sources = sources_ref[...]
    rows, cols = matrix_ref.shape
    lands = one_hot(sources - grid_row() * rows == iota((rows, width), 0))
    landed = half_dot(lands, jnp.ones((width, 128), HALF))
    kept_ref[...] = jnp.where(jnp.concatenate([landed] * (cols // 128), axis=1) > 0.5, 0.0, matrix_ref[...])

    sources_column = as_column(sources)
    square = (width, width)
    chosen = one_hot(sources_column == iota(square, 1))
    used = half_dot(jnp.ones((8, width), HALF), chosen)
    before = one_hot(iota(square, 0) <= iota(square, 1))
    free = 1.0 - used
    free_rank = half_dot(free.astype(HALF), before)
    vacated = jnp.broadcast_to(jnp.where(sources >= width, 1.0, 0.0), (8, width))
    vacated_rank = half_dot(vacated.astype(HALF), before)
    rank_column = jnp.transpose(vacated_rank)[:, 0:1]
    match = (free_rank[0:1] == rank_column) & (free[0:1] > 0.5) & (sources_column >= width)
    choose_ref[...] = chosen + one_hot(match)


def finish_kernel(
    sources_ref, got_ref, kept_ref, below_ref, inverse_ref, weights_ref, choose_ref, out_hbm, out_ref, sems
):
    rows, cols = kept_ref.shape
    width = sources_ref.shape[1]
    myself = grid_row()
    sources = sources_ref[...]
    moved = half_dot(choose_ref[...], got_ref[:, :, cols : 2 * cols].reshape(width, cols)).astype(HALF)
    found = got_ref[:, :, 0:cols].reshape(width, cols)
    pivots = jnp.where(as_column(sources) >= width, found, moved)
    count = width // 128
    upper = []
    for block in range(count):
        right = pivots[128 * block : 128 * block + 128]
        sides = jnp.concatenate([inverse_ref[0, block], inverse_ref[1, block]], axis=1)
        upper.append(half_dot(sides, jnp.concatenate([right, right], axis=0)))
    first = 0
    for at in range(count - 1):
        more = count - 1 - at
        change = split_dot(below_ref[:, first : first + more].reshape(2, 128 * more, 128), upper[at])
        for block in range(more):
            upper[at + 1 + block] = upper[at + 1 + block] + change[128 * block : 128 * block + 128]
        first += more
    upper = jnp.concatenate(upper, axis=0)

    quarter = rows // 4
    copies = []
    for at in range(4):
        here = pl.ds(at * quarter, quarter)
        copies.append(pltpu.make_async_copy(out_ref.at[here], out_hbm.at[here], sems.at[at]))

    @pl.when(myself == 0)
    def _():
        for at in range(4):
            here = slice(at * quarter, at * quarter + quarter)
            out_ref[here, :] = upper[here]
            copies[at].start()

    @pl.when(myself != 0)
    def _():
        half = upper.astype(HALF)
        for at in range(4):
            here = slice(at * quarter, at * quarter + quarter)
            lands = one_hot(sources - (myself * rows + at * quarter) == iota((quarter, width), 0))
            change = half_dot(lands, moved) + half_dot(weights_ref[here, :], half)
            out_ref[here, :] = kept_ref[here, :] + change
            copies[at].start()

    for copy in copies:
        copy.wait()


def everyone(block, count):
    return jnp.broadcast_to(block[None], (count,) + block.shape)


def exchange(blocks, axes):
    return lax.all_to_all(blocks, axes, 0, 0, tiled=False)


def on_device(matrix, panel, sources):
    rows, cols = matrix.shape
    width = sources.shape[0]
    parts = lax.axis_size(GRID_ROW)
    chips = lax.axis_size("y")
    each = width // parts
    f32 = jnp.float32
    sources = sources.reshape(1, width)
    columns = panel.T
    vmem = pl.BlockSpec(memory_space=pltpu.VMEM)
    hbm = pl.BlockSpec(memory_space=pltpu.HBM)

    offer, own = call(
        offer_kernel,
        (jax.ShapeDtypeStruct((parts, each, cols + 128), f32), jax.ShapeDtypeStruct(columns.shape, HALF)),
        2 * width * rows * cols,
        2 * rows * cols * 4,
        in_specs=[hbm, hbm, hbm],
        scratch_shapes=[
            pltpu.VMEM((1, width), jnp.int32),
            pltpu.VMEM((rows, cols), f32),
            pltpu.VMEM(columns.shape, f32),
            pltpu.SemaphoreType.DMA((6,)),
        ],
    )(in_hbm(sources), in_hbm(matrix), in_hbm(columns))
    got = exchange(offer.astype(SHORT), PARTNERS)

    choose, kept = call(
        choose_kernel,
        (jax.ShapeDtypeStruct((width, width), HALF), jax.ShapeDtypeStruct((rows, cols), f32)),
        4 * width * width * width,
        4 * rows * cols * 4,
    )(sources, matrix)

    def bring(block, ahead):
        return lax.ppermute(block, "y", [(i, (i - ahead) % chips) for i in range(chips)])

    came = [bring(own, 4), bring(own, 2)]
    piece = got[0, :, cols:]
    piece, came, choose, kept = lax.optimization_barrier((piece, came, choose, kept))
    mine = exchange(everyone(piece, 8 * chips), ("y", "x"))

    collected = call(
        collect_kernel, jax.ShapeDtypeStruct((parts, each, 2 * cols), HALF), parts * each * cols, 4 * parts * each * cols
    )(got.astype(f32))
    three = jnp.concatenate([own] + came, axis=0)
    came = bring(three, 1)
    collected, mine, came = lax.optimization_barrier((collected, mine, came))
    last = bring(jnp.concatenate([own, came[0:32]], axis=0), 6)
    arrived = exchange(collected, PARTNERS)
    other = lax.ppermute(mine, "core", [(0, 1), (1, 0)])

    below, inverse = call(
        invert_kernel,
        (jax.ShapeDtypeStruct((2, 6, 128, 128), HALF), jax.ShapeDtypeStruct((2, 4, 128, 128), HALF)),
        10 * width * width * width,
        8 * width * width * 4,
        scratch_shapes=[pltpu.VMEM((width, width), f32)],
    )(mine.astype(f32), other.astype(f32))
    last, inverse = lax.optimization_barrier((last, inverse))
    own = jnp.concatenate([three, came, last], axis=0)
    across = lax.ppermute(own, "core", [(0, 1), (1, 0)])
    weights = call(
        weights_kernel,
        jax.ShapeDtypeStruct((rows, width), HALF),
        width * rows,
        4 * width * rows,
        scratch_shapes=[pltpu.VMEM((width, rows), HALF)],
    )(own, across)
    return call(
        finish_kernel,
        jax.ShapeDtypeStruct((rows, cols), f32),
        8 * rows * cols * width,
        12 * rows * cols * 4,
        in_specs=[vmem] * 7,
        out_specs=hbm,
        scratch_shapes=[pltpu.VMEM((rows, cols), f32), pltpu.SemaphoreType.DMA((4,))],
    )(sources, arrived, kept, below, inverse, weights, choose)


def solution(mesh):
    shape = mesh.devices.shape
    chips = mesh.devices.reshape(shape[0] // 8, 8, shape[1] // 2, 2)
    grid = Mesh(chips, ("z", "x", "y", "core"))
    spec = P(GRID_ROW, ("y", "core"))
    return jax.shard_map(on_device, mesh=grid, in_specs=(spec, spec, P()), out_specs=spec, check_vma=False)
```
